512 devices in a mesh: seq: 64 (over x, y, core), dp: 8 (over z).
Axes of the slice: x: 4, y: 8, z: 8, core: 2. Of those that a mesh axis runs over, the one named last changes fastest.
Arguments:
- queries: bfloat16 [8, 8192, 512], P('dp', 'seq'), may hold values from -6 to 6
- keys: bfloat16 [8, 8192, 512], P('dp', 'seq'), may hold values from -6 to 6
- values: bfloat16 [8, 8192, 512], P('dp', 'seq'), may hold values from -6 to 6
- gates: bfloat16 [8, 8192, 512], P('dp', 'seq'), may hold values from -6 to 6
- cotangent: bfloat16 [8, 8192, 512], P('dp', 'seq'), may hold values from -6 to 6
- lengths: int32 [8, 5], P('dp'), may hold values from 1 to 32, 64 in all within a row
- gain: float32 [512], replicated, may hold values from 0.5 to 1.5
- bias: float32 [512], replicated, may hold values from -3 to 3
Outputs:
- grad_queries: bfloat16 [8, 8192, 512], P('dp', 'seq')
- grad_keys: bfloat16 [8, 8192, 512], P('dp', 'seq')
- grad_values: bfloat16 [8, 8192, 512], P('dp', 'seq')
- grad_gates: bfloat16 [8, 8192, 512], P('dp', 'seq')
- grad_gain: float32 [512], replicated
- grad_bias: float32 [512], replicated
The draws below stay inside these ranges and needn't reach their ends.
Inputs may be any that keep to these rules, and one draw needn't show every extreme that they name: Each row of lengths sums to 64 and its largest entry is exactly 32; a user's last block holds a window of 128 of its candidates.
All inputs are finite; a program needn't handle non-finite values.
Results may differ from the reference program's by a relative error of at most 0.0058.
Values may be sent and summed in bfloat16 or wider, within the bound.
A program may use at most 64 MiB of HBM per device.

```python
import math
import jax
import jax.numpy as jnp
import numpy as np
from jax import lax

HEADS = 4
HD = 128
WIDTH = 512
BLOCK = 128
SPAN = 31
TOK_DEV = 128
TOKENS = 8192
NB = 64
MOST_BLK = 32
USERS = 5
N_DP = 8


def levels(key, dims, split, smallest, largest):
    def one(position, blocks):
        draws = jax.random.uniform(jax.random.fold_in(jax.random.fold_in(key, 6), position), (blocks,), jnp.float32, smallest / len(split), largest / len(split))
        return jnp.repeat(jnp.exp(draws), dims[position] // blocks).reshape((-1,) + (1,) * (len(dims) - position - 1))

    factor_of = one(*split[0])
    for cut in split[1:]:
        factor_of = factor_of * one(*cut)
    return factor_of


def profile(count, total, limit, lean):
    portions = [(1 << 20) // math.isqrt(rank ** lean) + 1 for rank in range(2, count + 1)]
    surplus, given = total - limit - (count - 1), [1] * (count - 1)
    while surplus > 0:
        movable = [i for i in range(count - 1) if given[i] < limit]
        whole, remaining = sum([portions[i] for i in movable]), surplus
        for i in movable:
            extra = min(limit - given[i], max(1, remaining * portions[i] // whole), surplus)
            given[i] = given[i] + extra
            surplus = surplus - extra
    return np.array([limit] + given)


def uneven_parts(key, count, total, reach, lean):
    if count == 2:
        one = jax.random.randint(key, (), max(1, total - reach), min(reach, total - 1) + 1)
        return jnp.stack([one, total - one])
    tallies = jnp.asarray(profile(count, total, reach, lean), jnp.int32)
    pairs = (count - 1) // 2
    source_of, sink = tallies[1:1 + 2 * pairs:2], tallies[2:2 + 2 * pairs:2]
    slack = jnp.minimum(source_of - 1, reach - sink)
    passed = jax.random.randint(jax.random.fold_in(key, 1), (pairs,), 0, 1 << 20) % (slack + 1)
    tallies = tallies.at[1:1 + 2 * pairs:2].set(source_of - passed).at[2:2 + 2 * pairs:2].set(sink + passed)
    return tallies[jax.random.permutation(jax.random.fold_in(key, 2), count)]


def normal_values(own_key, shape, width, bound, cuts=(), kind=jnp.bfloat16):
    drawn = width * jax.random.normal(own_key, shape, jnp.float32)
    if cuts:
        drawn = drawn * levels(own_key, shape, cuts, -0.22, 0.18)
    return jnp.clip(drawn, -bound, bound).astype(kind)


def setup_inputs(seed: int = 0) -> dict:
    seeds = jax.random.split(jax.random.key(seed), 9)
    return {
        "queries": normal_values(seeds[0], (N_DP, TOKENS, WIDTH), 1.0, 6.0, ((0, 8), (1, 64))),
        "keys": normal_values(seeds[1], (N_DP, TOKENS, WIDTH), 1.0, 6.0, ((0, 8), (1, 64))),
        "values": normal_values(seeds[2], (N_DP, TOKENS, WIDTH), 1.0, 6.0, ((0, 8), (1, 64))),
        "gates": normal_values(seeds[3], (N_DP, TOKENS, WIDTH), 1.0, 6.0, ((0, 8), (1, 64))),
        "cotangent": normal_values(seeds[4], (N_DP, TOKENS, WIDTH), 1.0, 6.0, ((0, 8), (1, 64))),
        "lengths": jax.vmap(lambda own: uneven_parts(own, USERS, NB, MOST_BLK, 2))(jax.random.split(seeds[5], N_DP)).reshape((N_DP, USERS)).astype(jnp.int32),
        "gain": jnp.clip(1.0 + 0.1 * jax.random.normal(seeds[6], (WIDTH,), jnp.float32), 0.5, 1.5),
        "bias": normal_values(seeds[7], (WIDTH,), 0.5, 3.0, (), jnp.float32),
    }


EPS = 1e-05

def row_info(lengths, places, total):
    ends = jnp.cumsum(lengths).astype(jnp.int32)
    blocks = places // BLOCK
    owner = lax.optimization_barrier(jnp.sum((blocks[:, None] >= ends[None, :]).astype(jnp.int32), axis=1)).astype(jnp.int32)
    final = jnp.any(blocks[:, None] + 1 == ends[None, :], axis=1)
    inside = (places >= 0) & (places < total)
    owner = jnp.where(inside, owner, -1).astype(jnp.int32)
    return (owner, final, places)

def pair_mask(query_info, key_info):
    query_owner, query_final, query_rows = query_info
    key_owner, key_final, key_rows = key_info
    same = (query_owner[:, None] == key_owner[None, :]) & (query_owner[:, None] >= 0)
    causal = key_rows[None, :] <= query_rows[:, None]
    allowed = jnp.logical_not(key_final[None, :]) | (key_rows[None, :] == query_rows[:, None])
    return same & causal & allowed

def heads_of(block):
    return block.astype(jnp.float32).reshape(block.shape[0], HEADS, HD)

def slice_info(info, start, count):
    return tuple((lax.dynamic_slice_in_dim(part, start, count, 0) for part in info))

def one_group(queries, keys, values, gates, cotangent, lengths, gain, bias):
    total = queries.shape[0]
    shards = total // TOK_DEV
    lead = SPAN * TOK_DEV
    window = (SPAN + 1) * TOK_DEV
    scale = HD ** (-0.5)
    own_info = row_info(lengths, jnp.arange(total, dtype=jnp.int32), total)
    key_info = row_info(lengths, jnp.arange(-lead, total, dtype=jnp.int32), total)
    padding = jnp.zeros((lead, WIDTH), keys.dtype)
    keys_pad = jnp.concatenate([padding, keys], axis=0)
    values_pad = jnp.concatenate([padding, values], axis=0)

    def pieces(index):
        start = (index * TOK_DEV).astype(jnp.int32)
        query_block = lax.dynamic_slice_in_dim(queries, start, TOK_DEV, 0)
        key_block = lax.dynamic_slice_in_dim(keys_pad, start, window, 0)
        value_block = lax.dynamic_slice_in_dim(values_pad, start, window, 0)
        mask = pair_mask(slice_info(own_info, start, TOK_DEV), slice_info(key_info, start, window))
        scores = jnp.einsum('qhd,khd->hqk', heads_of(query_block), heads_of(key_block)) * scale
        return (start, query_block, key_block, value_block, mask, scores)

    def forward(index):
        start, query_block, key_block, value_block, mask, scores = pieces(index)
        sigma = jax.nn.sigmoid(scores)
        probs = jnp.where(mask[None], scores * sigma, 0.0).astype(jnp.bfloat16)
        mixed = jnp.einsum('hqk,khd->qhd', probs.astype(jnp.float32), heads_of(value_block))
        return mixed.reshape(TOK_DEV, WIDTH)
    attended = lax.map(forward, jnp.arange(shards, dtype=jnp.int32)).reshape(total, WIDTH)
    mean = lax.optimization_barrier(jnp.mean(attended, axis=-1, keepdims=True))
    centered = attended - mean
    variance = lax.optimization_barrier(jnp.mean(centered * centered, axis=-1, keepdims=True))
    inverse = lax.rsqrt(variance + EPS)
    normal = centered * inverse
    scaled = normal * gain + bias
    cot_float = cotangent.astype(jnp.float32)
    upstream_norm = cot_float * gates.astype(jnp.float32)
    grad_gates = (cot_float * scaled).astype(jnp.bfloat16)
    gain_term = lax.optimization_barrier(jnp.sum(upstream_norm * normal, axis=0))
    bias_term = lax.optimization_barrier(jnp.sum(upstream_norm, axis=0))
    dnormal = upstream_norm * gain
    grad_attended = inverse * (dnormal - lax.optimization_barrier(jnp.mean(dnormal, axis=-1, keepdims=True)) - normal * lax.optimization_barrier(jnp.mean(dnormal * normal, axis=-1, keepdims=True)))
    grad_attended = grad_attended.astype(jnp.bfloat16)

    def backward(carry, index):
        key_sums, value_sums = carry
        start, query_block, key_block, value_block, mask, scores = pieces(index)
        upstream = lax.dynamic_slice_in_dim(grad_attended, start, TOK_DEV, 0)
        sigma = jax.nn.sigmoid(scores)
        probs = jnp.where(mask[None], scores * sigma, 0.0).astype(jnp.bfloat16)
        deriv = sigma * (1.0 + scores * (1.0 - sigma))
        pressure = jnp.einsum('qhd,khd->hqk', heads_of(upstream), heads_of(value_block))
        grad_scores = jnp.where(mask[None], pressure * deriv * scale, 0.0).astype(jnp.bfloat16)
        grad_query = jnp.einsum('hqk,khd->qhd', grad_scores.astype(jnp.float32), heads_of(key_block))
        grad_key = jnp.einsum('hqk,qhd->khd', grad_scores.astype(jnp.float32), heads_of(query_block))
        grad_value = jnp.einsum('hqk,qhd->khd', probs.astype(jnp.float32), heads_of(upstream))
        old_keys = lax.dynamic_slice_in_dim(key_sums, start, window, 0)
        old_values = lax.dynamic_slice_in_dim(value_sums, start, window, 0)
        key_sums = lax.dynamic_update_slice_in_dim(key_sums, old_keys + grad_key.reshape(window, WIDTH), start, 0)
        value_sums = lax.dynamic_update_slice_in_dim(value_sums, old_values + grad_value.reshape(window, WIDTH), start, 0)
        return ((key_sums, value_sums), grad_query.reshape(TOK_DEV, WIDTH).astype(jnp.bfloat16))
    empty = jnp.zeros((lead + total, WIDTH), jnp.float32)
    (key_sums, value_sums), grad_blocks = lax.scan(backward, (empty, empty), jnp.arange(shards, dtype=jnp.int32))
    grad_queries = grad_blocks.reshape(total, WIDTH)
    grad_keys = key_sums[lead:].astype(jnp.bfloat16)
    grad_values = value_sums[lead:].astype(jnp.bfloat16)
    return (grad_queries, grad_keys, grad_values, grad_gates, gain_term, bias_term)

def reference(queries, keys, values, gates, cotangent, lengths, gain, bias):

    def group(items):
        return one_group(items[0], items[1], items[2], items[3], items[4], items[5], gain, bias)
    results = lax.map(group, (queries, keys, values, gates, cotangent, lengths))
    grad_queries, grad_keys, grad_values, grad_gates, gain_terms, bias_terms = results
    norm_scale = 1.0 / math.sqrt(N_DP * TOKENS)
    grad_gain = lax.optimization_barrier(jnp.sum(gain_terms, axis=0)) * norm_scale
    grad_bias = lax.optimization_barrier(jnp.sum(bias_terms, axis=0)) * norm_scale
    return (grad_queries, grad_keys, grad_values, grad_gates, grad_gain, grad_bias)
```

```python
import math

import jax
import jax.numpy as jnp
from jax import lax
from jax.experimental import pallas as pl
from jax.experimental.pallas import tpu as pltpu
from jax.sharding import PartitionSpec as P

MESH = pl.DeviceIdType.MESH
NX = 4
NY = 8
HD = 128
EPS = 1e-05
USERS = 5

F32 = jnp.float32
BF16 = jnp.bfloat16


def dot(a, b):
    return lax.dot_general(a, b, (((1,), (0,)), ((), ())), preferred_element_type=F32)


def dot_t(a, b):
    return lax.dot_general(a, b, (((1,), (1,)), ((), ())), preferred_element_type=F32)


def make_kernel(nz, rows):
    pairs = NY // 2
    halves = pairs // 2
    stripe = 2 * NY
    heads = NY // 2
    width = heads * HD
    tile_q = 2 * rows
    tile_k = 4 * rows
    scale = HD ** (-0.5)
    norm_scale = 1.0 / math.sqrt(nz * NX * stripe * rows)

    def kernel(
        lengths, q_ref, k_ref, v_ref, gates_ref, cot_ref, gain_ref, bias_ref,
        gq_ref, gk_ref, gv_ref, gg_ref, gn_ref,
        qbuf, kvbuf, probs, derivs, att_acc, att_out, att_in, up, dabuf, q_t, da_t,
        dq_out, dq_in, dk_t, keep, sib_out, sib_in, x_out, x_in, fin, gk_in, gv_in,
        ysum, xsum, csum, zsum,
        q_s, q_r, k_s, k_r, v_s, v_r, f_s, f_r, att_s, att_r, da_s, da_r, dq_s, dq_r,
        sib_s, sib_r, xo_s, xo_r, fk_s, fk_r, fv_s, fv_r,
        ys_s, ys_r, xs_s, xs_r, cs_s, cs_r, zs_s, zs_r,
    ):
        me = lax.axis_index("seq")
        z = lax.axis_index("dp")
        x = me // stripe
        y = (me % stripe) // 2
        c = me % 2
        head = y // 2
        par = y % 2
        mine = y // 2

        def at(xx, yy, cc):
            return {"seq": (xx * NY + yy) * 2 + cc}

        sibling = at(x, y, 1 - c)

        def copy(src, dst, send, recv, target):
            return pltpu.make_async_remote_copy(
                src_ref=src, dst_ref=dst, send_sem=send, recv_sem=recv,
                device_id=target, device_id_type=MESH,
            )

        def arrived(dst, send, recv):
            copy(dst, dst, send, recv, sibling).wait_recv()

        def sent(src, send, recv):
            copy(src, src, send, recv, sibling).wait_send()

        def cols(h):
            return pl.ds(pl.multiple_of(h * HD, HD), HD)

        barrier = pltpu.get_barrier_semaphore()
        partners = [at(x, (y + d) % NY, c) for d in range(1, NY)]
        partners += [at((x + d) % NX, y, c) for d in range(1, NX)]
        partners += [sibling]
        partners += [{"dp": (z + d) % nz} for d in range(1, nz)]
        for partner in partners:
            pl.semaphore_signal(barrier, inc=1, device_id=partner, device_id_type=MESH)
        pl.semaphore_wait(barrier, len(partners))

        kvbuf[0, mine, c, :, 0:HD] = k_ref[:, cols(head)]
        kvbuf[0, mine, c, :, HD:2 * HD] = v_ref[:, cols(head)]
        for d in range(2, NY, 2):
            yy = (y + d) % NY
            copy(
                k_ref.at[:, cols(yy // 2)], kvbuf.at[0, mine, c, :, pl.ds(0, HD)],
                k_s.at[d // 2], k_r.at[mine], at(x, yy, c),
            ).start()
            copy(
                v_ref.at[:, cols(yy // 2)], kvbuf.at[0, mine, c, :, pl.ds(HD, HD)],
                v_s.at[d // 2], v_r.at[mine], at(x, yy, c),
            ).start()
        for d in range(1, NY):
            yy = (y + d) % NY
            copy(
                q_ref.at[:, cols(yy // 2)], qbuf.at[y], q_s.at[d], q_r.at[y], at(x, yy, c)
            ).start()
        qbuf[y] = q_ref[:, cols(head)]

        def forward_block(k):
            block = kvbuf.at[0, k, c]
            copy(block, block, f_s.at[0, k], f_r.at[0, k], sibling).start()

            @pl.when(x < NX - 1)
            def _():
                copy(block, kvbuf.at[1, k, c], f_s.at[1, k], f_r.at[1, k], at((x + 1) % NX, y, c)).start()

            @pl.when(x < NX - 2)
            def _():
                copy(block, kvbuf.at[2, k, c], f_s.at[2, k], f_r.at[2, k], at((x + 2) % NX, y, c)).start()

        forward_block(mine)
        for d in range(1, pairs):
            k = (mine + d) % pairs
            arrived(kvbuf.at[0, k, c, :, pl.ds(0, HD)], k_s.at[0], k_r.at[k])
            arrived(kvbuf.at[0, k, c, :, pl.ds(HD, HD)], v_s.at[0], v_r.at[k])
            forward_block(k)

        ends = []
        running = jnp.int32(0)
        for u in range(USERS):
            running = running + lengths[u]
            ends.append(running)

        def begin_of(block):
            begin = jnp.int32(0)
            last = jnp.int32(0)
            for end in ends:
                begin = jnp.maximum(begin, jnp.where(end <= block, end, 0))
                last = jnp.maximum(last, jnp.where(end == block + 1, 1, 0))
            return begin, last

        row = lax.broadcasted_iota(jnp.int32, (tile_q, 1), 0)
        second = row >= rows
        column = lax.broadcasted_iota(jnp.int32, (1, tile_k), 1)
        column = (column // (2 * rows)) * (4 * rows) + column % (2 * rows)

        def forward_body(t, m, half):
            first = stripe * x + c + 4 * m
            begin0, last0 = begin_of(first)
            begin1, last1 = begin_of(first + 2)
            begin = jnp.where(second, begin1, begin0) * rows
            at_key = column + (stripe * (x - t) + 2 * par + 8 * half) * rows
            allowed = at_key >= begin
            if t == 0:
                at_query = row + jnp.where(second, rows, 0) + first * rows
                last = jnp.where(second, last1, last0)
                start = jnp.where(second, first + 2, first) * rows
                limit = jnp.where(last == 1, start - 1, at_query)
                allowed = allowed & ((at_key <= limit) | (at_key == at_query))
            queries = qbuf[pl.ds(2 * m, 2)].reshape(tile_q, HD)
            keys = kvbuf[t, pl.ds(2 * half, 2), :, :, 0:HD].reshape(tile_k, HD)
            vals = kvbuf[t, pl.ds(2 * half, 2), :, :, HD:2 * HD].reshape(tile_k, HD)
            small = dot_t(queries, keys) * (0.5 * scale)
            up1 = jnp.tanh(small) + 1.0
            prob = small * up1
            deriv = (up1 + prob * (2.0 - up1)) * (0.5 * scale)
            prob = jnp.where(allowed, prob, 0.0).astype(BF16)
            slot = (t * pairs + m) * halves + half
            probs[slot] = prob
            derivs[slot] = jnp.where(allowed, deriv, 0.0).astype(BF16)
            att_acc[m] += dot(prob, vals)

        def spans(t, m):
            if t == 0:
                return 0, m // 2 + 1
            if t == 1:
                return 0, halves
            return m // 2, halves

        def sweep(t, body, first=0, last=pairs):
            def step(m, _):
                low, high = spans(t, m)
                lax.fori_loop(low, high, lambda half, _: body(t, m, half), None)

            lax.fori_loop(first, last, step, None)

        att_acc[...] = jnp.zeros_like(att_acc)
        for d in range(1, NY):
            slot = (y + d) % NY
            arrived(qbuf.at[slot], q_s.at[0], q_r.at[slot])
        for k in range(pairs):
            arrived(kvbuf.at[0, k, 1 - c], f_s.at[0, k], f_r.at[0, k])
        sweep(0, forward_body)

        for t in (1, 2):
            @pl.when(x >= t)
            def _(t=t):
                for k in range(pairs):
                    block = kvbuf.at[t, k, c]
                    arrived(block, f_s.at[t, k], f_r.at[t, k])
                    copy(block, block, f_s.at[t + 2, k], f_r.at[t + 2, k], sibling).start()
                for k in range(pairs):
                    arrived(kvbuf.at[t, k, 1 - c], f_s.at[t + 2, k], f_r.at[t + 2, k])
                sweep(t, forward_body)

        def to_owner(slot, source, landing, send, recv):
            there = landing.at[par, :, cols(head)]

            @pl.when(slot == y)
            def _():
                landing[par, :, cols(head)] = source[slot]

            @pl.when(slot != y)
            def _():
                copy(source.at[slot], there, send.at[slot], recv.at[y], at(x, slot, c)).start()

        for m in range(pairs):
            att_out[2 * m] = att_acc[m, 0:rows].astype(BF16)
            att_out[2 * m + 1] = att_acc[m, rows:2 * rows].astype(BF16)
            to_owner(2 * m, att_out, att_in, att_s, att_r)
            to_owner(2 * m + 1, att_out, att_in, att_s, att_r)

        for m in range(pairs):
            q_t[m] = qbuf[2 * m:2 * m + 2].reshape(tile_q, HD).T

        def gather_owner(landing, send, recv):
            for d in range(1, NY):
                yy = (y + d) % NY
                arrived(landing.at[yy % 2, :, cols(yy // 2)], send.at[0], recv.at[yy])

        gather_owner(att_in, att_s, att_r)
        attended = att_in[0].astype(F32) + att_in[1].astype(F32)
        mean = jnp.mean(attended, axis=-1, keepdims=True)
        centered = attended - mean
        variance = jnp.mean(centered * centered, axis=-1, keepdims=True)
        inverse = lax.rsqrt(variance + EPS)
        normal = centered * inverse
        gain = gain_ref[...]
        cot = cot_ref[...].astype(F32)
        upstream = cot * gates_ref[...].astype(F32)
        dnormal = upstream * gain
        grad_att = inverse * (
            dnormal
            - jnp.mean(dnormal, axis=-1, keepdims=True)
            - normal * jnp.mean(dnormal * normal, axis=-1, keepdims=True)
        )
        up[...] = grad_att.astype(BF16)
        for d in range(1, NY):
            yy = (y + d) % NY
            copy(up.at[:, cols(yy // 2)], dabuf.at[y], da_s.at[d], da_r.at[y], at(x, yy, c)).start()
        dabuf[y] = up[:, cols(head)]
        gg_ref[...] = (cot * (normal * gain + bias_ref[...])).astype(BF16)
        ysum[y, 0:1] = jnp.sum(upstream * normal, axis=0, keepdims=True)
        ysum[y, 1:2] = jnp.sum(upstream, axis=0, keepdims=True)

        def spread(buf, index, count, send, recv, target):
            for d in range(1, count):
                copy(buf.at[index], buf.at[index], send.at[d], recv.at[index], target(d)).start()

        def total(buf, index, count, send, recv):
            for d in range(1, count):
                other = (index + d) % count
                arrived(buf.at[other], send.at[0], recv.at[other])
            result = buf[0]
            for i in range(1, count):
                result = result + buf[i]
            return result

        spread(ysum, y, NY, ys_s, ys_r, lambda d: at(x, (y + d) % NY, c))

        att_acc[...] = jnp.zeros_like(att_acc)
        for d in range(1, NY):
            slot = (y + d) % NY
            arrived(dabuf.at[slot], da_s.at[0], da_r.at[slot])
        for m in range(pairs):
            da_t[m] = dabuf[2 * m:2 * m + 2].reshape(tile_q, HD).T

        def backward_body(t, m, half):
            slot = (t * pairs + m) * halves + half
            ups = dabuf[pl.ds(2 * m, 2)].reshape(tile_q, HD)
            keys = kvbuf[t, pl.ds(2 * half, 2), :, :, 0:HD].reshape(tile_k, HD)
            vals = kvbuf[t, pl.ds(2 * half, 2), :, :, HD:2 * HD].reshape(tile_k, HD)
            grads = (dot_t(ups, vals) * derivs[slot].astype(F32)).astype(BF16)
            att_acc[m] += dot(grads, keys)
            dk_t[half, 0:HD] += dot(q_t[m], grads)
            dk_t[half, HD:2 * HD] += dot(da_t[m], probs[slot])

        def split_cores(t):
            for k in range(pairs):
                part = dk_t[k // 2, :, (k % 2) * 2 * rows:(k % 2 + 1) * 2 * rows].T
                upper, lower = part[0:rows], part[rows:2 * rows]

                @pl.when(c == 0)
                def _(k=k, upper=upper, lower=lower):
                    keep[t, k] = upper
                    sib_out[t, k] = lower.astype(BF16)

                @pl.when(c == 1)
                def _(k=k, upper=upper, lower=lower):
                    keep[t, k] = lower
                    sib_out[t, k] = upper.astype(BF16)

            copy(sib_out.at[t], sib_in.at[t], sib_s.at[t], sib_r.at[t], sibling).start()

        def send_back(t):
            arrived(sib_in.at[t], sib_s.at[t], sib_r.at[t])
            x_out[t - 1] = (keep[t] + sib_in[t].astype(F32)).astype(BF16)
            copy(
                x_out.at[t - 1], x_in.at[t - 1], xo_s.at[t - 1], xo_r.at[t - 1],
                at((x + NX - t) % NX, y, c),
            ).start()

        @pl.when(x >= 2)
        def _():
            dk_t[...] = jnp.zeros_like(dk_t)
            sweep(2, backward_body)
            split_cores(2)

        @pl.when(x >= 1)
        def _():
            dk_t[...] = jnp.zeros_like(dk_t)
            sweep(1, backward_body, 0, pairs // 2)

        @pl.when(x >= 2)
        def _():
            send_back(2)

        @pl.when(x >= 1)
        def _():
            sweep(1, backward_body, pairs // 2, pairs)
            split_cores(1)

        xsum[x] = total(ysum, y, NY, ys_s, ys_r)
        spread(xsum, x, NX, xs_s, xs_r, lambda d: at((x + d) % NX, y, c))

        dk_t[...] = jnp.zeros_like(dk_t)
        sweep(0, backward_body, 0, pairs // 2)

        @pl.when(x >= 1)
        def _():
            send_back(1)

        def dq_pair(m):
            dq_out[2 * m] = att_acc[m, 0:rows].astype(BF16)
            dq_out[2 * m + 1] = att_acc[m, rows:2 * rows].astype(BF16)
            to_owner(2 * m, dq_out, dq_in, dq_s, dq_r)
            to_owner(2 * m + 1, dq_out, dq_in, dq_s, dq_r)

        for m in range(pairs // 2):
            dq_pair(m)
        sweep(0, backward_body, pairs // 2, pairs)
        split_cores(0)
        for m in range(pairs // 2, pairs):
            dq_pair(m)

        csum[c] = total(xsum, x, NX, xs_s, xs_r)
        spread(csum, c, 2, cs_s, cs_r, lambda d: sibling)

        arrived(sib_in.at[0], sib_s.at[0], sib_r.at[0])
        keep[0] = keep[0] + sib_in[0].astype(F32)
        for t in (1, 2):
            @pl.when(x < NX - t)
            def _(t=t):
                arrived(x_in.at[t - 1], xo_s.at[t - 1], xo_r.at[t - 1])
                keep[0] = keep[0] + x_in[t - 1].astype(F32)
        fin[...] = keep[0].astype(BF16)
        for d in range(1, pairs):
            k = (mine + d) % pairs
            yy = par + 2 * k
            copy(fin.at[k, :, pl.ds(0, HD)], gk_in.at[:, cols(head)], fk_s.at[d], fk_r.at[head], at(x, yy, c)).start()
            copy(fin.at[k, :, pl.ds(HD, HD)], gv_in.at[:, cols(head)], fv_s.at[d], fv_r.at[head], at(x, yy, c)).start()
        gk_in[:, cols(head)] = fin[mine, :, 0:HD]
        gv_in[:, cols(head)] = fin[mine, :, HD:2 * HD]

        zsum[z] = total(csum, c, 2, cs_s, cs_r)
        spread(zsum, z, nz, zs_s, zs_r, lambda d: {"dp": (z + d) % nz})

        gather_owner(dq_in, dq_s, dq_r)
        gq_ref[...] = (dq_in[0].astype(F32) + dq_in[1].astype(F32)).astype(BF16)
        for d in range(1, heads):
            h = (head + d) % heads
            arrived(gk_in.at[:, cols(h)], fk_s.at[0], fk_r.at[h])
            arrived(gv_in.at[:, cols(h)], fv_s.at[0], fv_r.at[h])
        gk_ref[...] = gk_in[...]
        gv_ref[...] = gv_in[...]
        gn_ref[...] = total(zsum, z, nz, zs_s, zs_r) * norm_scale

        for d in range(2, NY, 2):
            sent(k_ref.at[:, cols(head)], k_s.at[d // 2], k_r.at[0])
            sent(v_ref.at[:, cols(head)], v_s.at[d // 2], v_r.at[0])
        for d in range(1, NY):
            sent(qbuf.at[0], q_s.at[d], q_r.at[0])
            sent(dabuf.at[0], da_s.at[d], da_r.at[0])
            slot = (y + d) % NY
            sent(att_out.at[slot], att_s.at[slot], att_r.at[0])
            sent(dq_out.at[slot], dq_s.at[slot], dq_r.at[0])
            sent(ysum.at[y], ys_s.at[d], ys_r.at[0])
        for k in range(pairs):
            sent(kvbuf.at[0, k, c], f_s.at[0, k], f_r.at[0, k])
        for t in (1, 2):
            @pl.when(x < NX - t)
            def _(t=t):
                for k in range(pairs):
                    sent(kvbuf.at[0, k, c], f_s.at[t, k], f_r.at[0, k])

            @pl.when(x >= t)
            def _(t=t):
                for k in range(pairs):
                    sent(kvbuf.at[t, k, c], f_s.at[t + 2, k], f_r.at[0, k])
                sent(sib_out.at[t], sib_s.at[t], sib_r.at[t])
                sent(x_out.at[t - 1], xo_s.at[t - 1], xo_r.at[t - 1])
        sent(sib_out.at[0], sib_s.at[0], sib_r.at[0])
        for d in range(1, pairs):
            k = (mine + d) % pairs
            sent(fin.at[k, :, pl.ds(0, HD)], fk_s.at[d], fk_r.at[0])
            sent(fin.at[k, :, pl.ds(HD, HD)], fv_s.at[d], fv_r.at[0])
        for d in range(1, NX):
            sent(xsum.at[x], xs_s.at[d], xs_r.at[0])
        sent(csum.at[c], cs_s.at[1], cs_r.at[0])
        for d in range(1, nz):
            sent(zsum.at[z], zs_s.at[d], zs_r.at[0])

    vm = pltpu.VMEM
    sem = pltpu.SemaphoreType.DMA
    scratch = [
        vm((NY, rows, HD), BF16),
        vm((3, pairs, 2, rows, 2 * HD), BF16),
        vm((3 * pairs * halves, tile_q, tile_k), BF16),
        vm((3 * pairs * halves, tile_q, tile_k), BF16),
        vm((pairs, tile_q, HD), F32),
        vm((NY, rows, HD), BF16),
        vm((2, rows, width), BF16),
        vm((rows, width), BF16),
        vm((NY, rows, HD), BF16),
        vm((pairs, HD, tile_q), BF16),
        vm((pairs, HD, tile_q), BF16),
        vm((NY, rows, HD), BF16),
        vm((2, rows, width), BF16),
        vm((halves, 2 * HD, tile_k), F32),
        vm((3, pairs, rows, 2 * HD), F32),
        vm((3, pairs, rows, 2 * HD), BF16),
        vm((3, pairs, rows, 2 * HD), BF16),
        vm((2, pairs, rows, 2 * HD), BF16),
        vm((2, pairs, rows, 2 * HD), BF16),
        vm((pairs, rows, 2 * HD), BF16),
        vm((rows, width), BF16),
        vm((rows, width), BF16),
        vm((NY, 2, width), F32),
        vm((NX, 2, width), F32),
        vm((2, 2, width), F32),
        vm((nz, 2, width), F32),
        sem((NY,)), sem((NY,)),
        sem((pairs,)), sem((pairs,)), sem((pairs,)), sem((pairs,)),
        sem((5, pairs)), sem((5, pairs)),
        sem((NY,)), sem((NY,)), sem((NY,)), sem((NY,)), sem((NY,)), sem((NY,)),
        sem((3,)), sem((3,)), sem((2,)), sem((2,)),
        sem((pairs,)), sem((pairs,)), sem((pairs,)), sem((pairs,)),
        sem((NY,)), sem((NY,)), sem((NX,)), sem((NX,)), sem((2,)), sem((2,)), sem((nz,)), sem((nz,)),
    ]
    out = jax.ShapeDtypeStruct((rows, width), BF16)
    whole = pl.BlockSpec(memory_space=pltpu.VMEM)
    return pl.pallas_call(
        kernel,
        out_shape=[out, out, out, out, jax.ShapeDtypeStruct((2, width), F32)],
        in_specs=[pl.BlockSpec(memory_space=pltpu.SMEM)] + [whole] * 7,
        out_specs=[whole] * 5,
        scratch_shapes=scratch,
        compiler_params=pltpu.CompilerParams(
            collective_id=0, has_side_effects=True, vmem_limit_bytes=40 * 1024 * 1024
        ),
    )


def solution(mesh):
    nz = mesh.shape["dp"]

    def per_device(queries, keys, values, gates, cotangent, lengths, gain, bias):
        gq, gk, gv, gg, gn = make_kernel(nz, queries.shape[1])(
            lengths[0], queries[0], keys[0], values[0], gates[0], cotangent[0], gain[None], bias[None]
        )
        return gq[None], gk[None], gv[None], gg[None], gn[0], gn[1]

    rows = P("dp", "seq", None)
    return jax.shard_map(
        per_device,
        mesh=mesh,
        in_specs=(rows, rows, rows, rows, rows, P("dp", None), P(), P()),
        out_specs=(rows, rows, rows, rows, P(), P()),
        check_vma=False,
    )
```

```python
import math

import jax
import jax.numpy as jnp
from jax import lax
from jax.experimental import pallas as pl
from jax.experimental.pallas import tpu as pltpu
from jax.sharding import PartitionSpec as P

MESH = pl.DeviceIdType.MESH
NX = 4
NY = 8
HD = 128
EPS = 1e-05
USERS = 5

F32 = jnp.float32
BF16 = jnp.bfloat16


def dot(a, b):
    return lax.dot_general(a, b, (((1,), (0,)), ((), ())), preferred_element_type=F32)


def dot_t(a, b):
    return lax.dot_general(a, b, (((1,), (1,)), ((), ())), preferred_element_type=F32)


def make_kernel(nz, rows):
    pairs = NY // 2
    halves = pairs // 2
    stripe = 2 * NY
    heads = NY // 2
    width = heads * HD
    tile_q = 2 * rows
    tile_k = 4 * rows
    scale = HD ** (-0.5)
    norm_scale = 1.0 / math.sqrt(nz * NX * stripe * rows)

    def kernel(
        lengths, q_ref, k_ref, v_ref, gates_ref, cot_ref, gain_ref, bias_ref,
        gq_ref, gk_ref, gv_ref, gg_ref, gn_ref,
        qbuf, kvbuf, gates, cots, probs, derivs, att_acc, att_out, att_in, up, dabuf, q_t, da_t,
        dq_acc, dq_out, dq_in, dk_t, keep, sib_out, sib_in, x_out, x_in, fin, gk_in, gv_in,
        ysum, xsum, csum, zsum, gq_out, gg_out, gn_out, marks,
        own_s, q_s, q_r, k_s, k_r, v_s, v_r, f_s, f_r, att_s, att_r, da_s, da_r, dq_s, dq_r,
        sib_s, sib_r, xo_s, xo_r, fk_s, fk_r, fv_s, fv_r,
        ys_s, ys_r, xs_s, xs_r, cs_s, cs_r, zs_s, zs_r, gn_r, out_s,
    ):
        me = lax.axis_index("seq")
        z = lax.axis_index("dp")
        x = me // stripe
        y = (me % stripe) // 2
        c = me % 2
        head = y // 2
        par = y % 2
        mine = y // 2

        def at(xx, yy, cc):
            return {"seq": (xx * NY + yy) * 2 + cc}

        sibling = at(x, y, 1 - c)

        def copy(src, dst, send, recv, target):
            return pltpu.make_async_remote_copy(
                src_ref=src, dst_ref=dst, send_sem=send, recv_sem=recv,
                device_id=target, device_id_type=MESH,
            )

        def arrived(dst, send, recv):
            copy(dst, dst, send, recv, sibling).wait_recv()

        def sent(src, send, recv):
            copy(src, src, send, recv, sibling).wait_send()

        def cols(h):
            return pl.ds(pl.multiple_of(h * HD, HD), HD)

        own = [
            pltpu.make_async_copy(k_ref.at[:, cols(head)], kvbuf.at[0, mine, c, :, pl.ds(0, HD)], own_s.at[0]),
            pltpu.make_async_copy(v_ref.at[:, cols(head)], kvbuf.at[0, mine, c, :, pl.ds(HD, HD)], own_s.at[1]),
            pltpu.make_async_copy(q_ref.at[:, cols(head)], qbuf.at[y], own_s.at[2]),
            pltpu.make_async_copy(gates_ref, gates, own_s.at[3]),
            pltpu.make_async_copy(cot_ref, cots, own_s.at[4]),
        ]
        for one in own:
            one.start()

        def store(index, here, there):
            pltpu.make_async_copy(here, there, out_s.at[index]).start()

        barrier = pltpu.get_barrier_semaphore()
        partners = [at(x, (y + d) % NY, c) for d in range(1, NY)]
        partners += [at((x + d) % NX, y, c) for d in range(1, NX)]
        partners += [sibling]
        for partner in partners:
            pl.semaphore_signal(barrier, inc=1, device_id=partner, device_id_type=MESH)

        @pl.when(z == 0)
        def _():
            for d in range(1, nz):
                pl.semaphore_signal(barrier, inc=1, device_id={"dp": d}, device_id_type=MESH)

        pl.semaphore_wait(barrier, len(partners) + jnp.where(z == 0, 0, 1))

        for d in range(2, NY, 2):
            yy = (y + d) % NY
            copy(
                k_ref.at[:, cols(yy // 2)], kvbuf.at[0, mine, c, :, pl.ds(0, HD)],
                k_s.at[d // 2], k_r.at[mine], at(x, yy, c),
            ).start()
            copy(
                v_ref.at[:, cols(yy // 2)], kvbuf.at[0, mine, c, :, pl.ds(HD, HD)],
                v_s.at[d // 2], v_r.at[mine], at(x, yy, c),
            ).start()
        def send_queries():
            for d in range(1, NY):
                yy = (y + d) % NY
                copy(
                    q_ref.at[:, cols(yy // 2)], qbuf.at[y], q_s.at[d], q_r.at[y], at(x, yy, c)
                ).start()

        pl.when(y >= NY // 2)(send_queries)

        def forward_block(k, t):
            block = kvbuf.at[0, k, c]

            @pl.when(x < NX - t)
            def _():
                copy(block, kvbuf.at[t, k, c], f_s.at[t, k], f_r.at[t, k], at((x + t) % NX, y, c)).start()

        def share_block(t, k):
            block = kvbuf.at[t, k, c]
            copy(block, block, f_s.at[3 + t, k], f_r.at[3 + t, k], sibling).start()

        def share_stripe(t):
            @pl.when(x >= t)
            def _():
                for k in range(pairs):
                    arrived(kvbuf.at[t, k, c], f_s.at[t, k], f_r.at[t, k])
                    share_block(t, k)

        def shared(t):
            for k in range(pairs):
                arrived(kvbuf.at[t, k, 1 - c], f_s.at[3 + t, k], f_r.at[3 + t, k])

        ends = []
        running = jnp.int32(0)
        for u in range(USERS):
            running = running + lengths[0, u]
            ends.append(running)
        for slot in range(NY):
            block = stripe * x + 2 * slot + c
            begin = jnp.int32(0)
            final = jnp.int32(0)
            for end in ends:
                begin = jnp.maximum(begin, jnp.where(end <= block, end, 0))
                final = jnp.maximum(final, jnp.where(end == block + 1, 1, 0))
            marks[0, slot] = begin * rows
            marks[1, slot] = jnp.where(final == 1, block, 2 * NX * stripe) * rows

        own[0].wait()
        own[1].wait()
        share_block(0, mine)
        forward_block(mine, 1)
        for d in range(1, pairs):
            k = (mine + d) % pairs
            arrived(kvbuf.at[0, k, c, :, pl.ds(0, HD)], k_s.at[0], k_r.at[k])
            arrived(kvbuf.at[0, k, c, :, pl.ds(HD, HD)], v_s.at[0], v_r.at[k])
            share_block(0, k)
            forward_block(k, 1)
        pl.when(y < NY // 2)(send_queries)
        for d in range(pairs):
            forward_block((mine + d) % pairs, 2)
        share_stripe(1)

        column = lax.broadcasted_iota(jnp.int32, (1, tile_k), 1)
        column = (column // (2 * rows)) * (4 * rows) + column % (2 * rows)
        grid_row = lax.broadcasted_iota(jnp.int32, (tile_q, tile_k), 0)
        grid_column = lax.broadcasted_iota(jnp.int32, (tile_q, tile_k), 1)
        grid_gap = (
            (grid_column // (2 * rows)) * (4 * rows) + grid_column % (2 * rows)
            - grid_row - jnp.where(grid_row >= rows, rows, 0)
        )

        def keys_of(t, half):
            return kvbuf[t, 2 * half:2 * half + 2, :, :, 0:HD].reshape(tile_k, HD)

        def values_of(t, half):
            return kvbuf[t, 2 * half:2 * half + 2, :, :, HD:2 * HD].reshape(tile_k, HD)

        def forward_tile(t, m, half):
            shift = (2 * par + 8 * half) * rows
            at_key = column + (stripe * (x - t) * rows + shift)
            inside = []
            for slot in (2 * m, 2 * m + 1):
                kept = at_key >= marks[0, slot]
                if t == 0 and half == m // 2:
                    kept = kept & (at_key < marks[1, slot])
                inside.append(jnp.broadcast_to(jnp.where(kept, 1.0, 0.0), (rows, tile_k)))
            inside = jnp.concatenate(inside, axis=0)
            if t == 0 and half == m // 2:
                gap = grid_gap + (shift - (c + 4 * m) * rows)
                inside = jnp.where(gap < 0, inside, jnp.where(gap == 0, 1.0, 0.0))
            queries = qbuf[2 * m:2 * m + 2].reshape(tile_q, HD)
            small = dot_t(queries, keys_of(t, half)) * (0.5 * scale)
            twice = jnp.tanh(small) + 1.0
            weighed = twice * inside
            prob = small * weighed
            slot = (t * 2 + m // 2) * halves + half
            place = slice((m % 2) * tile_q, (m % 2 + 1) * tile_q)
            prob_low = prob.astype(BF16)
            probs[slot, place] = prob_low
            derivs[slot, place] = (weighed + prob * (2.0 - twice)).astype(BF16)
            return dot(prob_low, values_of(t, half))

        def spans(t, side):
            if t == 0:
                return range(0, side + 1)
            if t == 1:
                return range(0, halves)
            return range(side, halves)

        def forward_side(t, side):
            for m in (2 * side, 2 * side + 1):
                result = None
                for half in spans(t, side):
                    part = forward_tile(t, m, half)
                    result = part if result is None else result + part
                att_acc[m] = result if t == 0 else att_acc[m] + result

        def to_owner(slot, source, landing, send, recv):
            there = landing.at[par, :, cols(head)]

            @pl.when(slot == y)
            def _():
                landing[par, :, cols(head)] = source[slot]

            @pl.when(slot != y)
            def _():
                copy(source.at[slot], there, send.at[slot], recv.at[y], at(x, slot, c)).start()

        def attended_side(side):
            for m in (2 * side, 2 * side + 1):
                att_out[2 * m] = att_acc[m, 0:rows].astype(BF16)
                to_owner(2 * m, att_out, att_in, att_s, att_r)
                att_out[2 * m + 1] = att_acc[m, rows:2 * rows].astype(BF16)
                to_owner(2 * m + 1, att_out, att_in, att_s, att_r)

        def queries_here(side):
            for slot in range(4 * side, 4 * side + 4):
                @pl.when(slot == y)
                def _():
                    own[2].wait()

                @pl.when(slot != y)
                def _(slot=slot):
                    arrived(qbuf.at[slot], q_s.at[0], q_r.at[slot])

        queries_here(1)
        shared(0)
        forward_side(0, 1)

        @pl.when(x >= 1)
        def _():
            shared(1)
            forward_side(1, 1)

        queries_here(0)
        forward_side(0, 0)
        share_stripe(2)

        @pl.when(x >= 2)
        def _():
            shared(2)
            forward_side(2, 1)

        attended_side(1)

        @pl.when(x >= 1)
        def _():
            forward_side(1, 0)

        @pl.when(x >= 2)
        def _():
            forward_side(2, 0)

        attended_side(0)

        def transposed(source, target):
            for m in range(pairs):
                block = source[2 * m:2 * m + 2].reshape(tile_q, HD)
                target[m // 2, :, (m % 2) * tile_q:(m % 2 + 1) * tile_q] = block.T

        def gather_owner(landing, send, recv):
            for d in range(1, NY):
                yy = (y + d) % NY
                arrived(landing.at[yy % 2, :, cols(yy // 2)], send.at[0], recv.at[yy])

        dq_acc[...] = jnp.zeros_like(dq_acc)
        transposed(qbuf, q_t)
        own[3].wait()
        own[4].wait()
        gain = gain_ref[...]
        cot = cots[...].astype(F32)
        upstream = cot * gates[...].astype(F32)
        dnormal = upstream * gain
        dnormal_mean = jnp.mean(dnormal, axis=-1, keepdims=True)
        ysum[y, 1:2] = jnp.sum(upstream, axis=0, keepdims=True)

        gather_owner(att_in, att_s, att_r)
        attended = att_in[0].astype(F32) + att_in[1].astype(F32)
        mean = jnp.mean(attended, axis=-1, keepdims=True)
        centered = attended - mean
        variance = jnp.mean(centered * centered, axis=-1, keepdims=True)
        inverse = lax.rsqrt(variance + EPS)
        normal = centered * inverse
        grad_att = inverse * (
            dnormal - dnormal_mean - normal * jnp.mean(dnormal * normal, axis=-1, keepdims=True)
        )
        up[...] = grad_att.astype(BF16)
        for d in range(1, NY):
            yy = (y + d) % NY
            copy(up.at[:, cols(yy // 2)], dabuf.at[y], da_s.at[d], da_r.at[y], at(x, yy, c)).start()
        dabuf[y] = up[:, cols(head)]
        ysum[y, 0:1] = jnp.sum(upstream * normal, axis=0, keepdims=True)

        def spread(buf, index, count, send, recv, target):
            for d in range(1, count):
                copy(buf.at[index], buf.at[index], send.at[d], recv.at[index], target(d)).start()

        def total(buf, index, count, send, recv):
            for d in range(1, count):
                other = (index + d) % count
                arrived(buf.at[other], send.at[0], recv.at[other])
            result = buf[0]
            for i in range(1, count):
                result = result + buf[i]
            return result

        spread(ysum, y, NY, ys_s, ys_r, lambda d: at(x, (y + d) % NY, c))
        gg_out[...] = (cot * (normal * gain + bias_ref[...])).astype(BF16)
        store(3, gg_out, gg_ref)

        for d in range(1, NY):
            slot = (y + d) % NY
            arrived(dabuf.at[slot], da_s.at[0], da_r.at[slot])
        transposed(dabuf, da_t)

        def backward_tile(t, side, half, fresh):
            slot = (t * 2 + side) * halves + half
            ups = dabuf[4 * side:4 * side + 4].reshape(2 * tile_q, HD)
            pressure = dot_t(ups, values_of(t, half))
            grads = (pressure * derivs[slot].astype(F32)).astype(BF16)
            dq_acc[side] += dot(grads, keys_of(t, half))
            part_k = dot(q_t[side], grads)
            part_v = dot(da_t[side], probs[slot])
            if fresh:
                dk_t[t, half, 0:HD] = part_k
                dk_t[t, half, HD:2 * HD] = part_v
            else:
                dk_t[t, half, 0:HD] += part_k
                dk_t[t, half, HD:2 * HD] += part_v

        def split_cores(t, half):
            for k in (2 * half, 2 * half + 1):
                there = slice((k % 2) * 2 * rows, (k % 2 + 1) * 2 * rows)
                part = jnp.concatenate(
                    [(dk_t[t, half, 0:HD, there] * (0.5 * scale)).T, dk_t[t, half, HD:2 * HD, there].T], axis=1
                )
                upper, lower = part[0:rows], part[rows:2 * rows]

                @pl.when(c == 0)
                def _(k=k, upper=upper, lower=lower):
                    keep[t, k] = upper
                    sib_out[t, k] = lower.astype(BF16)

                @pl.when(c == 1)
                def _(k=k, upper=upper, lower=lower):
                    keep[t, k] = lower
                    sib_out[t, k] = upper.astype(BF16)

            some = pl.ds(2 * half, 2)
            copy(sib_out.at[t, some], sib_in.at[t, some], sib_s.at[t, half], sib_r.at[t, half], sibling).start()

        def send_back(t, half):
            some = pl.ds(2 * half, 2)
            arrived(sib_in.at[t, some], sib_s.at[t, half], sib_r.at[t, half])
            x_out[t - 1, some] = (keep[t, some] + sib_in[t, some].astype(F32)).astype(BF16)
            copy(
                x_out.at[t - 1, some], x_in.at[t - 1, some], xo_s.at[t - 1, half], xo_r.at[t - 1, half],
                at((x + NX - t) % NX, y, c),
            ).start()

        def grad_queries_side(side):
            for m in (2 * side, 2 * side + 1):
                first = (m % 2) * tile_q
                part = dq_acc[side, first:first + rows] * (0.5 * scale)
                dq_out[2 * m] = part.astype(BF16)
                to_owner(2 * m, dq_out, dq_in, dq_s, dq_r)
                part = dq_acc[side, first + rows:first + 2 * rows] * (0.5 * scale)
                dq_out[2 * m + 1] = part.astype(BF16)
                to_owner(2 * m + 1, dq_out, dq_in, dq_s, dq_r)

        @pl.when(x >= 2)
        def _():
            backward_tile(2, 0, 0, True)
            split_cores(2, 0)
            backward_tile(2, 0, 1, True)
            backward_tile(2, 1, 1, False)
            split_cores(2, 1)

        xsum[x] = total(ysum, y, NY, ys_s, ys_r)
        spread(xsum, x, NX, xs_s, xs_r, lambda d: at((x + d) % NX, y, c))

        @pl.when(x >= 2)
        def _():
            send_back(2, 0)

        @pl.when(x >= 1)
        def _():
            backward_tile(1, 0, 0, True)
            backward_tile(1, 1, 0, False)
            split_cores(1, 0)

        @pl.when(x >= 2)
        def _():
            send_back(2, 1)

        @pl.when(x >= 1)
        def _():
            backward_tile(1, 0, 1, True)
            backward_tile(1, 1, 1, False)
            split_cores(1, 1)
            send_back(1, 0)

        backward_tile(0, 0, 0, True)
        grad_queries_side(0)

        @pl.when(x >= 1)
        def _():
            send_back(1, 1)

        backward_tile(0, 1, 0, False)
        split_cores(0, 0)
        backward_tile(0, 1, 1, True)
        split_cores(0, 1)
        grad_queries_side(1)

        csum[c] = total(xsum, x, NX, xs_s, xs_r)
        spread(csum, c, 2, cs_s, cs_r, lambda d: sibling)

        for half in range(halves):
            some = pl.ds(2 * half, 2)
            arrived(sib_in.at[0, some], sib_s.at[0, half], sib_r.at[0, half])
            keep[0, some] = keep[0, some] + sib_in[0, some].astype(F32)

        zsum[z] = total(csum, c, 2, cs_s, cs_r)

        @pl.when(z > 0)
        def _():
            copy(zsum.at[z], zsum.at[z], zs_s.at[0], zs_r.at[z], {"dp": 0}).start()

        for half in range(halves):
            some = pl.ds(2 * half, 2)
            for t in (1, 2):
                @pl.when(x < NX - t)
                def _(t=t, some=some, half=half):
                    arrived(x_in.at[t - 1, some], xo_s.at[t - 1, half], xo_r.at[t - 1, half])
                    keep[0, some] = keep[0, some] + x_in[t - 1, some].astype(F32)
            fin[some] = keep[0, some].astype(BF16)
            for k in (2 * half, 2 * half + 1):
                yy = par + 2 * k

                @pl.when(k == mine)
                def _(k=k):
                    gk_in[:, cols(head)] = fin[k, :, 0:HD]
                    gv_in[:, cols(head)] = fin[k, :, HD:2 * HD]

                @pl.when(k != mine)
                def _(k=k, yy=yy):
                    copy(fin.at[k, :, pl.ds(0, HD)], gk_in.at[:, cols(head)], fk_s.at[k], fk_r.at[head], at(x, yy, c)).start()
                    copy(fin.at[k, :, pl.ds(HD, HD)], gv_in.at[:, cols(head)], fv_s.at[k], fv_r.at[head], at(x, yy, c)).start()

        gather_owner(dq_in, dq_s, dq_r)
        gq_out[...] = (dq_in[0].astype(F32) + dq_in[1].astype(F32)).astype(BF16)
        store(0, gq_out, gq_ref)

        @pl.when(z == 0)
        def _():
            result = zsum[0]
            for i in range(1, nz):
                arrived(zsum.at[i], zs_s.at[0], zs_r.at[i])
                result = result + zsum[i]
            gn_out[...] = result * norm_scale
            for i in range(1, nz):
                copy(gn_out, gn_out, zs_s.at[i], gn_r.at[0], {"dp": i}).start()

        for d in range(2, NY, 2):
            sent(k_ref.at[:, cols(head)], k_s.at[d // 2], k_r.at[0])
            sent(v_ref.at[:, cols(head)], v_s.at[d // 2], v_r.at[0])
        for d in range(1, NY):
            sent(qbuf.at[0], q_s.at[d], q_r.at[0])
            sent(dabuf.at[0], da_s.at[d], da_r.at[0])
            slot = (y + d) % NY
            sent(att_out.at[slot], att_s.at[slot], att_r.at[0])
            sent(dq_out.at[slot], dq_s.at[slot], dq_r.at[0])
            sent(ysum.at[y], ys_s.at[d], ys_r.at[0])
        for k in range(pairs):
            sent(kvbuf.at[0, k, c], f_s.at[3, k], f_r.at[0, k])
        for t in (1, 2):
            @pl.when(x < NX - t)
            def _(t=t):
                for k in range(pairs):
                    sent(kvbuf.at[0, k, c], f_s.at[t, k], f_r.at[0, k])

            @pl.when(x >= t)
            def _(t=t):
                for k in range(pairs):
                    sent(kvbuf.at[t, k, c], f_s.at[3 + t, k], f_r.at[0, k])
                for half in range(halves):
                    some = pl.ds(2 * half, 2)
                    sent(sib_out.at[t, some], sib_s.at[t, half], sib_r.at[t, half])
                    sent(x_out.at[t - 1, some], xo_s.at[t - 1, half], xo_r.at[t - 1, half])
        for half in range(halves):
            some = pl.ds(2 * half, 2)
            sent(sib_out.at[0, some], sib_s.at[0, half], sib_r.at[0, half])
        for d in range(1, NX):
            sent(xsum.at[x], xs_s.at[d], xs_r.at[0])
        sent(csum.at[c], cs_s.at[1], cs_r.at[0])

        @pl.when(z > 0)
        def _():
            sent(zsum.at[z], zs_s.at[0], zs_r.at[0])

        @pl.when(z == 0)
        def _():
            for i in range(1, nz):
                sent(gn_out, zs_s.at[i], zs_r.at[0])

        for d in range(1, heads):
            h = (head + d) % heads
            arrived(gk_in.at[:, cols(h)], fk_s.at[0], fk_r.at[h])
            arrived(gv_in.at[:, cols(h)], fv_s.at[0], fv_r.at[h])
        store(1, gk_in, gk_ref)
        store(2, gv_in, gv_ref)

        @pl.when(z > 0)
        def _():
            arrived(gn_out, zs_s.at[0], gn_r.at[0])

        store(4, gn_out, gn_ref)
        for d in range(1, pairs):
            k = (mine + d) % pairs
            sent(fin.at[k, :, pl.ds(0, HD)], fk_s.at[k], fk_r.at[0])
            sent(fin.at[k, :, pl.ds(HD, HD)], fv_s.at[k], fv_r.at[0])
        for i, (here, there) in enumerate(
            [(gq_out, gq_ref), (gk_in, gk_ref), (gv_in, gv_ref), (gg_out, gg_ref), (gn_out, gn_ref)]
        ):
            pltpu.make_async_copy(here, there, out_s.at[i]).wait()

    vm = pltpu.VMEM
    sem = pltpu.SemaphoreType.DMA
    scratch = [
        vm((NY, rows, HD), BF16),
        vm((3, pairs, 2, rows, 2 * HD), BF16),
        vm((rows, width), BF16),
        vm((rows, width), BF16),
        vm((6 * halves, 2 * tile_q, tile_k), BF16),
        vm((6 * halves, 2 * tile_q, tile_k), BF16),
        vm((pairs, tile_q, HD), F32),
        vm((NY, rows, HD), BF16),
        vm((2, rows, width), BF16),
        vm((rows, width), BF16),
        vm((NY, rows, HD), BF16),
        vm((2, HD, 2 * tile_q), BF16),
        vm((2, HD, 2 * tile_q), BF16),
        vm((2, 2 * tile_q, HD), F32),
        vm((NY, rows, HD), BF16),
        vm((2, rows, width), BF16),
        vm((3, halves, 2 * HD, tile_k), F32),
        vm((3, pairs, rows, 2 * HD), F32),
        vm((3, pairs, rows, 2 * HD), BF16),
        vm((3, pairs, rows, 2 * HD), BF16),
        vm((2, pairs, rows, 2 * HD), BF16),
        vm((2, pairs, rows, 2 * HD), BF16),
        vm((pairs, rows, 2 * HD), BF16),
        vm((rows, width), BF16),
        vm((rows, width), BF16),
        vm((NY, 2, width), F32),
        vm((NX, 2, width), F32),
        vm((2, 2, width), F32),
        vm((nz, 2, width), F32),
        vm((rows, width), BF16),
        vm((rows, width), BF16),
        vm((2, width), F32),
        pltpu.SMEM((2, NY), jnp.int32),
        sem((5,)),
        sem((NY,)), sem((NY,)),
        sem((pairs,)), sem((pairs,)), sem((pairs,)), sem((pairs,)),
        sem((6, pairs)), sem((6, pairs)),
        sem((NY,)), sem((NY,)), sem((NY,)), sem((NY,)), sem((NY,)), sem((NY,)),
        sem((3, halves)), sem((3, halves)), sem((2, halves)), sem((2, halves)),
        sem((pairs,)), sem((pairs,)), sem((pairs,)), sem((pairs,)),
        sem((NY,)), sem((NY,)), sem((NX,)), sem((NX,)), sem((2,)), sem((2,)), sem((nz,)), sem((nz,)), sem((1,)),
        sem((5,)),
    ]
    out = jax.ShapeDtypeStruct((rows, width), BF16)
    whole = pl.BlockSpec(memory_space=pltpu.VMEM)
    far = pl.BlockSpec(memory_space=pltpu.HBM)
    return pl.pallas_call(
        kernel,
        out_shape=[out, out, out, out, jax.ShapeDtypeStruct((2, width), F32)],
        in_specs=[pl.BlockSpec(memory_space=pltpu.SMEM)] + [far] * 5 + [whole] * 2,
        out_specs=[far] * 5,
        scratch_shapes=scratch,
        compiler_params=pltpu.CompilerParams(
            collective_id=0, has_side_effects=True, vmem_limit_bytes=63 * 1024 * 1024
        ),
    )


def write_out(*refs):
    arrays, outs, held, sems = refs[0:5], refs[5:11], refs[11:16], refs[16]
    loads = [pltpu.make_async_copy(arrays[i], held[i], sems.at[i]) for i in range(5)]
    places = list(held[0:4]) + [held[4].at[0], held[4].at[1]]
    stores = [pltpu.make_async_copy(places[i], outs[i], sems.at[5 + i]) for i in range(6)]
    for load in loads:
        load.start()
    for i in range(4):
        loads[i].wait()
        stores[i].start()
    loads[4].wait()
    stores[4].start()
    stores[5].start()
    for store in stores:
        store.wait()


def written(*arrays):
    far = pl.BlockSpec(memory_space=pltpu.HBM)
    gn = arrays[4]
    row = jax.ShapeDtypeStruct(gn.shape[1:], gn.dtype)
    return pl.pallas_call(
        write_out,
        out_shape=[jax.ShapeDtypeStruct(one.shape, one.dtype) for one in arrays[0:4]] + [row, row],
        in_specs=[far] * 5,
        out_specs=[far] * 6,
        scratch_shapes=[pltpu.VMEM(one.shape, one.dtype) for one in arrays] + [pltpu.SemaphoreType.DMA((11,))],
        compiler_params=pltpu.CompilerParams(vmem_limit_bytes=63 * 1024 * 1024),
    )(*arrays)


def solution(mesh):
    nz = mesh.shape["dp"]

    def per_device(queries, keys, values, gates, cotangent, lengths, gain, bias):
        gq, gk, gv, gg, gn = make_kernel(nz, queries.shape[1])(
            lengths, queries[0], keys[0], values[0], gates[0], cotangent[0], gain[None], bias[None]
        )
        gq, gk, gv, gg, gain_grad, bias_grad = written(gq, gk, gv, gg, gn)
        return gq[None], gk[None], gv[None], gg[None], gain_grad, bias_grad

    rows = P("dp", "seq", None)
    return jax.shard_map(
        per_device,
        mesh=mesh,
        in_specs=(rows, rows, rows, rows, rows, P("dp", None), P(), P()),
        out_specs=(rows, rows, rows, rows, P(), P()),
        check_vma=False,
    )
```

```python
import math

import jax
import jax.numpy as jnp
from jax import lax
from jax.experimental import pallas as pl
from jax.experimental.pallas import tpu as pltpu
from jax.sharding import PartitionSpec as P

MESH = pl.DeviceIdType.MESH
NX = 4
NY = 8
HD = 128
EPS = 1e-05
USERS = 5

F32 = jnp.float32
BF16 = jnp.bfloat16


def dot(a, b):
    return lax.dot_general(a, b, (((1,), (0,)), ((), ())), preferred_element_type=F32)


def dot_t(a, b):
    return lax.dot_general(a, b, (((1,), (1,)), ((), ())), preferred_element_type=F32)


def make_kernel(nz, rows):
    pairs = NY // 2
    halves = pairs // 2
    stripe = 2 * NY
    heads = NY // 2
    width = heads * HD
    tile_q = 2 * rows
    tile_k = 4 * rows
    scale = HD ** (-0.5)
    norm_scale = 1.0 / math.sqrt(nz * NX * stripe * rows)

    def kernel(
        lengths, q_ref, k_ref, v_ref, gates_ref, cot_ref, gain_ref, bias_ref,
        gq_ref, gk_ref, gv_ref, gg_ref, gn_ref,
        qbuf, kvbuf, gates, cots, probs, derivs, att_acc, att_out, att_in, up, dabuf, q_t, da_t,
        dq_acc, dq_out, dq_in, dk_t, keep, sib_out, sib_in, x_out, x_in, fin,
        ysum, xsum, csum, zsum, gq_out, gg_out, gn_out, gains, biases, relay, mid_in, pass_in, marks, counts,
        own_s, r_s, r_r, mid_r, pass_s, pass_r, q_s, q_r, k_s, k_r, v_s, v_r, f_s, f_r, att_s, att_r, da_s, da_r, dq_s, dq_r,
        sib_s, sib_r, xo_s, xo_r, fk_s, fk_r, fv_s, fv_r,
        ys_s, ys_r, xs_s, xs_r, cs_s, cs_r, zs_s, zs_r, gn_r, out_s,
    ):
        me = lax.axis_index("seq")
        z = lax.axis_index("dp")
        x = me // stripe
        y = (me % stripe) // 2
        c = me % 2
        head = y // 2
        par = y % 2
        mine = y // 2

        def at(xx, yy, cc):
            return {"seq": (xx * NY + yy) * 2 + cc}

        sibling = at(x, y, 1 - c)

        def copy(src, dst, send, recv, target):
            return pltpu.make_async_remote_copy(
                src_ref=src, dst_ref=dst, send_sem=send, recv_sem=recv,
                device_id=target, device_id_type=MESH,
            )

        def arrived(dst, send, recv):
            copy(dst, dst, send, recv, sibling).wait_recv()

        def sent(src, send, recv):
            copy(src, src, send, recv, sibling).wait_send()

        def cols(h):
            return pl.ds(pl.multiple_of(h * HD, HD), HD)

        far_first = sorted(range(1, NY), key=lambda d: -min(d, NY - d))
        own = [
            pltpu.make_async_copy(k_ref.at[:, cols(head)], kvbuf.at[0, mine, c, :, pl.ds(0, HD)], own_s.at[0]),
            pltpu.make_async_copy(v_ref.at[:, cols(head)], kvbuf.at[0, mine, c, :, pl.ds(HD, HD)], own_s.at[1]),
            pltpu.make_async_copy(q_ref.at[:, cols(head)], qbuf.at[y], own_s.at[2]),
            pltpu.make_async_copy(gates_ref, gates, own_s.at[3]),
            pltpu.make_async_copy(cot_ref, cots, own_s.at[4]),
            pltpu.make_async_copy(lengths, counts, own_s.at[5]),
            pltpu.make_async_copy(gain_ref, gains, own_s.at[6]),
            pltpu.make_async_copy(bias_ref, biases, own_s.at[7]),
        ]
        for one in own:
            one.start()

        def store(index, here, there):
            pltpu.make_async_copy(here, there, out_s.at[index]).start()

        barrier = pltpu.get_barrier_semaphore()
        partners = [at(x, (y + d) % NY, c) for d in range(1, NY)]
        partners += [at((x + d) % NX, y, c) for d in range(1, NX)]
        partners += [sibling]
        for partner in partners:
            pl.semaphore_signal(barrier, inc=1, device_id=partner, device_id_type=MESH)

        @pl.when(z == 0)
        def _():
            for d in range(1, nz):
                pl.semaphore_signal(barrier, inc=1, device_id={"dp": d}, device_id_type=MESH)

        pl.semaphore_wait(barrier, len(partners) + jnp.where(z == 0, 0, 1))

        for d in far_first:
            if d % 2:
                continue
            yy = (y + d) % NY
            copy(
                k_ref.at[:, cols(yy // 2)], kvbuf.at[0, mine, c, :, pl.ds(0, HD)],
                k_s.at[d // 2], k_r.at[mine], at(x, yy, c),
            ).start()
            copy(
                v_ref.at[:, cols(yy // 2)], kvbuf.at[0, mine, c, :, pl.ds(HD, HD)],
                v_s.at[d // 2], v_r.at[mine], at(x, yy, c),
            ).start()
        for d in far_first:
            yy = (y + d) % NY
            copy(q_ref.at[:, cols(yy // 2)], qbuf.at[y], q_s.at[d], q_r.at[y], at(x, yy, c)).start()

        def forward_block(k):
            block = kvbuf.at[0, k, c]

            @pl.when(x < NX - 1)
            def _():
                copy(block, kvbuf.at[1, k, c], f_s.at[1, k], f_r.at[1, k], at((x + 1) % NX, y, c)).start()

            @pl.when((x < NX - 2) & (k % 2 == 1))
            def _():
                copy(block, relay.at[k // 2], r_s.at[k // 2], r_r.at[k // 2], at((x + NX - 1) % NX, y, c)).start()

        def forward_again(block, k, target):
            copy(block, kvbuf.at[2, k, c], f_s.at[2, k], f_r.at[2, k], at(target, y, c)).start()

        def share_block(t, k):
            block = kvbuf.at[t, k, c]
            copy(block, block, f_s.at[3 + t, k], f_r.at[3 + t, k], sibling).start()

        def share_stripe(t):
            @pl.when(x >= t)
            def _():
                for k in range(pairs):
                    arrived(kvbuf.at[t, k, c], f_s.at[t, k], f_r.at[t, k])
                    share_block(t, k)
                    if t == 1 and k % 2 == 0:
                        @pl.when(x < NX - 1)
                        def _(k=k):
                            forward_again(kvbuf.at[1, k, c], k, (x + 1) % NX)

        def shared(t):
            for k in range(pairs):
                arrived(kvbuf.at[t, k, 1 - c], f_s.at[3 + t, k], f_r.at[3 + t, k])

        for i in (5, 6, 7):
            own[i].wait()
        ends = []
        running = jnp.int32(0)
        for u in range(USERS):
            running = running + counts[0, u]
            ends.append(running)
        for slot in range(NY):
            block = stripe * x + 2 * slot + c
            begin = jnp.int32(0)
            final = jnp.int32(0)
            for end in ends:
                begin = jnp.maximum(begin, jnp.where(end <= block, end, 0))
                final = jnp.maximum(final, jnp.where(end == block + 1, 1, 0))
            marks[0, slot] = begin * rows
            marks[1, slot] = jnp.where(final == 1, block, 2 * NX * stripe) * rows

        own[0].wait()
        own[1].wait()
        share_block(0, mine)
        forward_block(mine)
        for d in range(1, pairs):
            k = (mine + d) % pairs
            arrived(kvbuf.at[0, k, c, :, pl.ds(0, HD)], k_s.at[0], k_r.at[k])
            arrived(kvbuf.at[0, k, c, :, pl.ds(HD, HD)], v_s.at[0], v_r.at[k])
            share_block(0, k)
            forward_block(k)

        @pl.when((x == 0) | (x == NX - 1))
        def _():
            for i in range(halves):
                arrived(relay.at[i], r_s.at[i], r_r.at[i])
                forward_again(relay.at[i], 2 * i + 1, (x + NX - 1) % NX)

        share_stripe(1)

        column = lax.broadcasted_iota(jnp.int32, (1, tile_k), 1)
        column = (column // (2 * rows)) * (4 * rows) + column % (2 * rows)
        grid_row = lax.broadcasted_iota(jnp.int32, (tile_q, tile_k), 0)
        grid_column = lax.broadcasted_iota(jnp.int32, (tile_q, tile_k), 1)
        grid_gap = (
            (grid_column // (2 * rows)) * (4 * rows) + grid_column % (2 * rows)
            - grid_row - jnp.where(grid_row >= rows, rows, 0)
        )

        def keys_of(t, half):
            return kvbuf[t, 2 * half:2 * half + 2, :, :, 0:HD].reshape(tile_k, HD)

        def values_of(t, half):
            return kvbuf[t, 2 * half:2 * half + 2, :, :, HD:2 * HD].reshape(tile_k, HD)

        def forward_tile(t, m, half):
            shift = (2 * par + 8 * half) * rows
            at_key = column + (stripe * (x - t) * rows + shift)
            inside = []
            for slot in (2 * m, 2 * m + 1):
                kept = at_key >= marks[0, slot]
                if t == 0 and half == m // 2:
                    kept = kept & (at_key < marks[1, slot])
                inside.append(jnp.broadcast_to(jnp.where(kept, 1.0, 0.0), (rows, tile_k)))
            inside = jnp.concatenate(inside, axis=0)
            if t == 0 and half == m // 2:
                gap = grid_gap + (shift - (c + 4 * m) * rows)
                inside = jnp.where(gap < 0, inside, jnp.where(gap == 0, 1.0, 0.0))
            queries = qbuf[2 * m:2 * m + 2].reshape(tile_q, HD)
            small = dot_t(queries, keys_of(t, half)) * (0.5 * scale)
            twice = jnp.tanh(small) + 1.0
            weighed = twice * inside
            prob = small * weighed
            slot = (t * 2 + m // 2) * halves + half
            place = slice((m % 2) * tile_q, (m % 2 + 1) * tile_q)
            prob_low = prob.astype(BF16)
            probs[slot, place] = prob_low
            derivs[slot, place] = (weighed + prob * (2.0 - twice)).astype(BF16)
            return dot(prob_low, values_of(t, half))

        def spans(t, m):
            if t == 0:
                return range(0, m // 2 + 1)
            if t == 1:
                return range(0, halves)
            return range(m // 2, halves)

        def forward_side(t, side):
            for m in range(side, pairs, 2):
                result = None
                for half in spans(t, m):
                    part = forward_tile(t, m, half)
                    result = part if result is None else result + part
                att_acc[m] = result if t == 0 else att_acc[m] + result

        def to_owner(slot, source, landing, send, recv):
            there = landing.at[par, :, cols(head)]

            @pl.when(slot == y)
            def _():
                landing[par, :, cols(head)] = source[slot]

            @pl.when(slot != y)
            def _():
                copy(source.at[slot], there, send.at[slot], recv.at[y], at(x, slot, c)).start()

        def attended_side(side):
            for m in range(side, pairs, 2):
                att_out[2 * m] = att_acc[m, 0:rows].astype(BF16)
                to_owner(2 * m, att_out, att_in, att_s, att_r)
                att_out[2 * m + 1] = att_acc[m, rows:2 * rows].astype(BF16)
                to_owner(2 * m + 1, att_out, att_in, att_s, att_r)

        def queries_here(side):
            for slot in range(4 * side, 4 * side + 4):
                @pl.when(slot == y)
                def _():
                    own[2].wait()

                @pl.when(slot != y)
                def _(slot=slot):
                    arrived(qbuf.at[slot], q_s.at[0], q_r.at[slot])

        queries_here(0)
        queries_here(1)
        shared(0)
        forward_side(0, 1)
        forward_side(0, 0)

        @pl.when(x >= 1)
        def _():
            shared(1)
            forward_side(1, 1)
            forward_side(1, 0)

        share_stripe(2)

        @pl.when(x >= 2)
        def _():
            shared(2)
            forward_side(2, 1)

        attended_side(1)

        @pl.when(x >= 2)
        def _():
            forward_side(2, 0)

        attended_side(0)

        def transposed(source, target):
            for m in range(pairs):
                block = source[2 * m:2 * m + 2].reshape(tile_q, HD)
                target[m // 2, :, (m % 2) * tile_q:(m % 2 + 1) * tile_q] = block.T

        def gather_owner(landing, send, recv):
            for d in range(1, NY):
                yy = (y + d) % NY
                arrived(landing.at[yy % 2, :, cols(yy // 2)], send.at[0], recv.at[yy])

        def spread(buf, index, count, send, recv, target):
            for d in range(1, count):
                copy(buf.at[index], buf.at[index], send.at[d], recv.at[index], target(d)).start()

        def total(buf, index, count, send, recv):
            for d in range(1, count):
                other = (index + d) % count
                arrived(buf.at[other], send.at[0], recv.at[other])
            result = buf[0]
            for i in range(1, count):
                result = result + buf[i]
            return result

        dq_acc[...] = jnp.zeros_like(dq_acc)
        transposed(qbuf, q_t)
        own[3].wait()
        own[4].wait()
        gain = gains[...]
        cot = cots[...].astype(F32)
        upstream = cot * gates[...].astype(F32)
        dnormal = upstream * gain
        dnormal_mean = jnp.mean(dnormal, axis=-1, keepdims=True)
        ysum[y, 1:2] = jnp.sum(upstream, axis=0, keepdims=True)

        gather_owner(att_in, att_s, att_r)
        attended = att_in[0].astype(F32) + att_in[1].astype(F32)
        mean = jnp.mean(attended, axis=-1, keepdims=True)
        centered = attended - mean
        variance = jnp.mean(centered * centered, axis=-1, keepdims=True)
        inverse = lax.rsqrt(variance + EPS)
        normal = centered * inverse
        grad_att = inverse * (
            dnormal - dnormal_mean - normal * jnp.mean(dnormal * normal, axis=-1, keepdims=True)
        )
        up[...] = grad_att.astype(BF16)
        ysum[y, 0:1] = jnp.sum(upstream * normal, axis=0, keepdims=True)
        spread(ysum, y, NY, ys_s, ys_r, lambda d: at(x, (y + d) % NY, c))
        for d in far_first:
            yy = (y + d) % NY
            copy(up.at[:, cols(yy // 2)], dabuf.at[y], da_s.at[d], da_r.at[y], at(x, yy, c)).start()
        dabuf[y] = up[:, cols(head)]
        gg_out[...] = (cot * (normal * gain + biases[...])).astype(BF16)
        store(3, gg_out, gg_ref)

        xsum[x] = total(ysum, y, NY, ys_s, ys_r)
        spread(xsum, x, NX, xs_s, xs_r, lambda d: at((x + d) % NX, y, c))

        for d in range(1, NY):
            slot = (y + d) % NY
            arrived(dabuf.at[slot], da_s.at[0], da_r.at[slot])
        transposed(dabuf, da_t)

        def backward_tile(t, side, half, fresh):
            slot = (t * 2 + side) * halves + half
            ups = dabuf[4 * side:4 * side + 4].reshape(2 * tile_q, HD)
            pressure = dot_t(ups, values_of(t, half))
            grads = (pressure * derivs[slot].astype(F32)).astype(BF16)
            dq_acc[side] += dot(grads, keys_of(t, half))
            part_k = dot(q_t[side], grads)
            part_v = dot(da_t[side], probs[slot])
            if fresh:
                dk_t[t, half, 0:HD] = part_k
                dk_t[t, half, HD:2 * HD] = part_v
            else:
                dk_t[t, half, 0:HD] += part_k
                dk_t[t, half, HD:2 * HD] += part_v

        def split_cores(t, half):
            for k in (2 * half, 2 * half + 1):
                there = slice((k % 2) * 2 * rows, (k % 2 + 1) * 2 * rows)
                part = jnp.concatenate(
                    [(dk_t[t, half, 0:HD, there] * (0.5 * scale)).T, dk_t[t, half, HD:2 * HD, there].T], axis=1
                )
                upper, lower = part[0:rows], part[rows:2 * rows]

                @pl.when(c == 0)
                def _(k=k, upper=upper, lower=lower):
                    keep[t, k] = upper
                    sib_out[t, k] = lower.astype(BF16)

                @pl.when(c == 1)
                def _(k=k, upper=upper, lower=lower):
                    keep[t, k] = lower
                    sib_out[t, k] = upper.astype(BF16)

            some = pl.ds(2 * half, 2)
            copy(sib_out.at[t, some], sib_in.at[t, some], sib_s.at[t, half], sib_r.at[t, half], sibling).start()

        turn = mine % 2

        def summed(t, k):
            return keep[t, k] + sib_in[t, k].astype(F32)

        def sibling_here(t, half):
            some = pl.ds(2 * half, 2)
            arrived(sib_in.at[t, some], sib_s.at[t, half], sib_r.at[t, half])

        def back_two(half):
            sibling_here(2, half)
            odd = 2 * half + turn
            even = 2 * half + 1 - turn
            x_out[1, even] = summed(2, even).astype(BF16)
            x_out[1, odd] = summed(2, odd).astype(BF16)
            copy(x_out.at[1, even], mid_in.at[half], xo_s.at[1, even], mid_r.at[half], at((x + NX - 1) % NX, y, c)).start()
            copy(x_out.at[1, odd], pass_in.at[half], xo_s.at[1, odd], pass_r.at[half], at((x + 1) % NX, y, c)).start()

        def back_one(k):
            copy(x_out.at[0, k], x_in.at[0, k], xo_s.at[0, k], xo_r.at[0, k], at((x + NX - 1) % NX, y, c)).start()

        def back_odd(half):
            sibling_here(1, half)
            odd = 2 * half + turn
            x_out[0, odd] = summed(1, odd).astype(BF16)
            back_one(odd)

        def back_even(half):
            even = 2 * half + 1 - turn
            keep[1, even] = summed(1, even)

            @pl.when(x < NX - 1)
            def _():
                arrived(mid_in.at[half], xo_s.at[1, 0], mid_r.at[half])
                keep[1, even] += mid_in[half].astype(F32)

            x_out[0, even] = keep[1, even].astype(BF16)
            back_one(even)

        def pass_back(half):
            arrived(pass_in.at[half], xo_s.at[1, 0], pass_r.at[half])
            copy(
                pass_in.at[half], x_in.at[1, 2 * half + turn], pass_s.at[half], xo_r.at[1, 2 * half + turn],
                at((x + 1) % NX, y, c),
            ).start()

        def grad_queries_side(side):
            for m in (2 * side, 2 * side + 1):
                first = (m % 2) * tile_q
                part = dq_acc[side, first:first + rows] * (0.5 * scale)
                dq_out[2 * m] = part.astype(BF16)
                to_owner(2 * m, dq_out, dq_in, dq_s, dq_r)
                part = dq_acc[side, first + rows:first + 2 * rows] * (0.5 * scale)
                dq_out[2 * m + 1] = part.astype(BF16)
                to_owner(2 * m + 1, dq_out, dq_in, dq_s, dq_r)

        @pl.when(x >= 2)
        def _():
            backward_tile(2, 0, 0, True)
            split_cores(2, 0)
            backward_tile(2, 0, 1, True)
            backward_tile(2, 1, 1, False)
            split_cores(2, 1)

        csum[c] = total(xsum, x, NX, xs_s, xs_r)
        spread(csum, c, 2, cs_s, cs_r, lambda d: sibling)

        @pl.when(x >= 2)
        def _():
            back_two(0)

        @pl.when(x >= 1)
        def _():
            backward_tile(1, 0, 0, True)
            backward_tile(1, 1, 0, False)
            split_cores(1, 0)

        @pl.when(x >= 2)
        def _():
            back_two(1)

        @pl.when(x >= 1)
        def _():
            backward_tile(1, 0, 1, True)
            backward_tile(1, 1, 1, False)
            split_cores(1, 1)
            back_odd(0)

        zsum[z] = total(csum, c, 2, cs_s, cs_r)

        @pl.when(z > 0)
        def _():
            copy(zsum.at[z], zsum.at[z], zs_s.at[0], zs_r.at[z], {"dp": 0}).start()

        backward_tile(0, 0, 0, True)
        grad_queries_side(0)

        @pl.when(x >= 1)
        def _():
            back_odd(1)
            back_even(0)

        backward_tile(0, 1, 0, False)
        split_cores(0, 0)

        @pl.when(x >= 1)
        def _():
            back_even(1)

        @pl.when(x == NX - 1)
        def _():
            for half in range(halves):
                pass_back(half)

        backward_tile(0, 1, 1, True)
        split_cores(0, 1)
        grad_queries_side(1)

        @pl.when(x == 0)
        def _():
            for half in range(halves):
                pass_back(half)

        for half in range(halves):
            some = pl.ds(2 * half, 2)
            arrived(sib_in.at[0, some], sib_s.at[0, half], sib_r.at[0, half])
            keep[0, some] = keep[0, some] + sib_in[0, some].astype(F32)

        for odd in (1, 0):
            for half in range(halves):
                k = (mine + 2 * half + 2 + 1 - odd) % pairs

                @pl.when(x < NX - 1)
                def _(k=k):
                    arrived(x_in.at[0, k], xo_s.at[0, k], xo_r.at[0, k])
                    keep[0, k] += x_in[0, k].astype(F32)

                if odd:
                    @pl.when(x < NX - 2)
                    def _(k=k):
                        arrived(x_in.at[1, k], xo_s.at[1, k], xo_r.at[1, k])
                        keep[0, k] += x_in[1, k].astype(F32)

                fin[k] = keep[0, k].astype(BF16)
                yy = par + 2 * k

                @pl.when(k == mine)
                def _(k=k):
                    pltpu.make_async_copy(fin.at[k, :, pl.ds(0, HD)], gk_ref.at[:, cols(head)], out_s.at[1]).start()
                    pltpu.make_async_copy(fin.at[k, :, pl.ds(HD, HD)], gv_ref.at[:, cols(head)], out_s.at[2]).start()

                @pl.when(k != mine)
                def _(k=k, yy=yy):
                    copy(fin.at[k, :, pl.ds(0, HD)], gk_ref.at[:, cols(head)], fk_s.at[k], fk_r.at[head], at(x, yy, c)).start()
                    copy(fin.at[k, :, pl.ds(HD, HD)], gv_ref.at[:, cols(head)], fv_s.at[k], fv_r.at[head], at(x, yy, c)).start()

        @pl.when(z == 0)
        def _():
            result = zsum[0]
            for i in range(1, nz):
                arrived(zsum.at[i], zs_s.at[0], zs_r.at[i])
                result = result + zsum[i]
            gn_out[...] = result * norm_scale
            for i in range(1, nz):
                copy(gn_out, gn_out, zs_s.at[i], gn_r.at[0], {"dp": i}).start()

        gather_owner(dq_in, dq_s, dq_r)
        gq_out[...] = (dq_in[0].astype(F32) + dq_in[1].astype(F32)).astype(BF16)
        store(0, gq_out, gq_ref)


        for d in range(2, NY, 2):
            sent(k_ref.at[:, cols(head)], k_s.at[d // 2], k_r.at[0])
            sent(v_ref.at[:, cols(head)], v_s.at[d // 2], v_r.at[0])
        for d in range(1, NY):
            sent(qbuf.at[0], q_s.at[d], q_r.at[0])
            sent(dabuf.at[0], da_s.at[d], da_r.at[0])
            slot = (y + d) % NY
            sent(att_out.at[slot], att_s.at[slot], att_r.at[0])
            sent(dq_out.at[slot], dq_s.at[slot], dq_r.at[0])
            sent(ysum.at[y], ys_s.at[d], ys_r.at[0])
        for k in range(pairs):
            sent(kvbuf.at[0, k, c], f_s.at[3, k], f_r.at[0, k])

        @pl.when(x < NX - 1)
        def _():
            for k in range(pairs):
                sent(kvbuf.at[0, k, c], f_s.at[1, k], f_r.at[0, k])

        @pl.when(x < NX - 2)
        def _():
            for i in range(halves):
                sent(relay.at[i], r_s.at[i], r_r.at[i])

        @pl.when((x == 0) | (x == NX - 1))
        def _():
            for half in range(halves):
                sent(pass_in.at[half], pass_s.at[half], pass_r.at[half])
            for k in range(1, pairs, 2):
                sent(kvbuf.at[0, k, c], f_s.at[2, k], f_r.at[0, k])

        @pl.when((x > 0) & (x < NX - 1))
        def _():
            for k in range(0, pairs, 2):
                sent(kvbuf.at[0, k, c], f_s.at[2, k], f_r.at[0, k])

        for t in (1, 2):
            @pl.when(x >= t)
            def _(t=t):
                for k in range(pairs):
                    sent(kvbuf.at[t, k, c], f_s.at[3 + t, k], f_r.at[0, k])
                for half in range(halves):
                    some = pl.ds(2 * half, 2)
                    sent(sib_out.at[t, some], sib_s.at[t, half], sib_r.at[t, half])
                for k in range(pairs):
                    sent(x_out.at[t - 1, k], xo_s.at[t - 1, k], xo_r.at[t - 1, k])
        for half in range(halves):
            some = pl.ds(2 * half, 2)
            sent(sib_out.at[0, some], sib_s.at[0, half], sib_r.at[0, half])
        for d in range(1, NX):
            sent(xsum.at[x], xs_s.at[d], xs_r.at[0])
        sent(csum.at[c], cs_s.at[1], cs_r.at[0])

        @pl.when(z > 0)
        def _():
            sent(zsum.at[z], zs_s.at[0], zs_r.at[0])

        @pl.when(z == 0)
        def _():
            for i in range(1, nz):
                sent(gn_out, zs_s.at[i], zs_r.at[0])

        for d in range(1, heads):
            h = (head + d) % heads
            arrived(gk_ref.at[:, cols(h)], fk_s.at[0], fk_r.at[h])
            arrived(gv_ref.at[:, cols(h)], fv_s.at[0], fv_r.at[h])
        @pl.when(z > 0)
        def _():
            arrived(gn_out, zs_s.at[0], gn_r.at[0])

        store(4, gn_out, gn_ref)
        for d in range(1, pairs):
            k = (mine + d) % pairs
            sent(fin.at[k, :, pl.ds(0, HD)], fk_s.at[k], fk_r.at[0])
            sent(fin.at[k, :, pl.ds(HD, HD)], fv_s.at[k], fv_r.at[0])
        for i, (here, there) in enumerate(
            [
                (gq_out, gq_ref),
                (fin.at[mine, :, pl.ds(0, HD)], gk_ref.at[:, cols(head)]),
                (fin.at[mine, :, pl.ds(HD, HD)], gv_ref.at[:, cols(head)]),
                (gg_out, gg_ref),
                (gn_out, gn_ref),
            ]
        ):
            pltpu.make_async_copy(here, there, out_s.at[i]).wait()

    vm = pltpu.VMEM
    sem = pltpu.SemaphoreType.DMA
    scratch = [
        vm((NY, rows, HD), BF16),
        vm((3, pairs, 2, rows, 2 * HD), BF16),
        vm((rows, width), BF16),
        vm((rows, width), BF16),
        vm((6 * halves, 2 * tile_q, tile_k), BF16),
        vm((6 * halves, 2 * tile_q, tile_k), BF16),
        vm((pairs, tile_q, HD), F32),
        vm((NY, rows, HD), BF16),
        vm((2, rows, width), BF16),
        vm((rows, width), BF16),
        vm((NY, rows, HD), BF16),
        vm((2, HD, 2 * tile_q), BF16),
        vm((2, HD, 2 * tile_q), BF16),
        vm((2, 2 * tile_q, HD), F32),
        vm((NY, rows, HD), BF16),
        vm((2, rows, width), BF16),
        vm((3, halves, 2 * HD, tile_k), F32),
        vm((3, pairs, rows, 2 * HD), F32),
        vm((3, pairs, rows, 2 * HD), BF16),
        vm((3, pairs, rows, 2 * HD), BF16),
        vm((2, pairs, rows, 2 * HD), BF16),
        vm((2, pairs, rows, 2 * HD), BF16),
        vm((pairs, rows, 2 * HD), BF16),
        vm((NY, 2, width), F32),
        vm((NX, 2, width), F32),
        vm((2, 2, width), F32),
        vm((nz, 2, width), F32),
        vm((rows, width), BF16),
        vm((rows, width), BF16),
        vm((2, width), F32),
        vm((1, width), F32),
        vm((1, width), F32),
        vm((halves, rows, 2 * HD), BF16),
        vm((halves, rows, 2 * HD), BF16),
        vm((halves, rows, 2 * HD), BF16),
        pltpu.SMEM((2, NY), jnp.int32),
        pltpu.SMEM((1, USERS), jnp.int32),
        sem((8,)), sem((halves,)), sem((halves,)), sem((halves,)), sem((halves,)), sem((halves,)),
        sem((NY,)), sem((NY,)),
        sem((pairs,)), sem((pairs,)), sem((pairs,)), sem((pairs,)),
        sem((6, pairs)), sem((6, pairs)),
        sem((NY,)), sem((NY,)), sem((NY,)), sem((NY,)), sem((NY,)), sem((NY,)),
        sem((3, halves)), sem((3, halves)), sem((2, pairs)), sem((2, pairs)),
        sem((pairs,)), sem((pairs,)), sem((pairs,)), sem((pairs,)),
        sem((NY,)), sem((NY,)), sem((NX,)), sem((NX,)), sem((2,)), sem((2,)), sem((nz,)), sem((nz,)), sem((1,)),
        sem((5,)),
    ]
    out = jax.ShapeDtypeStruct((rows, width), BF16)
    far = pl.BlockSpec(memory_space=pltpu.HBM)
    return pl.pallas_call(
        kernel,
        out_shape=[out, out, out, out, jax.ShapeDtypeStruct((2, width), F32)],
        in_specs=[far] * 8,
        out_specs=[far] * 5,
        scratch_shapes=scratch,
        compiler_params=pltpu.CompilerParams(
            collective_id=0, has_side_effects=True, vmem_limit_bytes=63 * 1024 * 1024
        ),
    )


def write_out(*refs):
    arrays, outs, held, sems = refs[0:5], refs[5:11], refs[11:16], refs[16]
    loads = [pltpu.make_async_copy(arrays[i], held[i], sems.at[i]) for i in range(5)]
    places = list(held[0:4]) + [held[4].at[0], held[4].at[1]]
    stores = [pltpu.make_async_copy(places[i], outs[i], sems.at[5 + i]) for i in range(6)]
    for load in loads:
        load.start()
    for i in range(4):
        loads[i].wait()
        stores[i].start()
    loads[4].wait()
    stores[4].start()
    stores[5].start()
    for store in stores:
        store.wait()


def written(*arrays):
    far = pl.BlockSpec(memory_space=pltpu.HBM)
    gn = arrays[4]
    row = jax.ShapeDtypeStruct(gn.shape[1:], gn.dtype)
    return pl.pallas_call(
        write_out,
        out_shape=[jax.ShapeDtypeStruct(one.shape, one.dtype) for one in arrays[0:4]] + [row, row],
        in_specs=[far] * 5,
        out_specs=[far] * 6,
        scratch_shapes=[pltpu.VMEM(one.shape, one.dtype) for one in arrays] + [pltpu.SemaphoreType.DMA((11,))],
        compiler_params=pltpu.CompilerParams(vmem_limit_bytes=63 * 1024 * 1024),
    )(*arrays)


def solution(mesh):
    nz = mesh.shape["dp"]

    def per_device(queries, keys, values, gates, cotangent, lengths, gain, bias):
        gq, gk, gv, gg, gn = make_kernel(nz, queries.shape[1])(
            lengths, queries[0], keys[0], values[0], gates[0], cotangent[0], gain[None], bias[None]
        )
        gq, gk, gv, gg, gain_grad, bias_grad = written(gq, gk, gv, gg, gn)
        return gq[None], gk[None], gv[None], gg[None], gain_grad, bias_grad

    rows = P("dp", "seq", None)
    return jax.shard_map(
        per_device,
        mesh=mesh,
        in_specs=(rows, rows, rows, rows, rows, P("dp", None), P(), P()),
        out_specs=(rows, rows, rows, rows, P(), P()),
        check_vma=False,
    )
```

```python
import math

import jax
import jax.numpy as jnp
from jax import lax
from jax.experimental import pallas as pl
from jax.experimental.pallas import tpu as pltpu
from jax.sharding import PartitionSpec as P

MESH = pl.DeviceIdType.MESH
NX = 4
NY = 8
HD = 128
EPS = 1e-05
USERS = 5

F32 = jnp.float32
BF16 = jnp.bfloat16


def dot(a, b):
    return lax.dot_general(a, b, (((1,), (0,)), ((), ())), preferred_element_type=F32)


def dot_t(a, b):
    return lax.dot_general(a, b, (((1,), (1,)), ((), ())), preferred_element_type=F32)


def make_kernel(nz, rows):
    pairs = NY // 2
    halves = pairs // 2
    stripe = 2 * NY
    heads = NY // 2
    width = heads * HD
    tile_q = 2 * rows
    tile_k = 4 * rows
    scale = HD ** (-0.5)
    norm_scale = 1.0 / math.sqrt(nz * NX * stripe * rows)

    def kernel(
        lengths, q_ref, k_ref, v_ref, gates_ref, cot_ref, gain_ref, bias_ref,
        gq_ref, gk_ref, gv_ref, gg_ref, gn_ref,
        qbuf, kvbuf, gates, cots, probs, derivs, att_acc, att_out, att_in, up, dabuf, q_t, da_t,
        dq_acc, dq_out, dq_in, dk_t, keep, sib_out, sib_in, x_out, x_in, fin,
        ysum, xsum, csum, zsum, gq_out, gg_out, gn_out, gains, biases, relay, mid_in, pass_in, marks, counts,
        own_s, r_s, r_r, mid_r, pass_s, pass_r, q_s, q_r, k_s, k_r, v_s, v_r, f_s, f_r, att_s, att_r, da_s, da_r, dq_s, dq_r,
        sib_s, sib_r, xo_s, xo_r, fk_s, fk_r, fv_s, fv_r,
        ys_s, ys_r, xs_s, xs_r, cs_s, cs_r, zs_s, zs_r, gn_r, out_s,
    ):
        me = lax.axis_index("seq")
        z = lax.axis_index("dp")
        x = me // stripe
        y = (me % stripe) // 2
        c = me % 2
        head = y // 2
        par = y % 2
        mine = y // 2

        def at(xx, yy, cc):
            return {"seq": (xx * NY + yy) * 2 + cc}

        sibling = at(x, y, 1 - c)

        def copy(src, dst, send, recv, target):
            return pltpu.make_async_remote_copy(
                src_ref=src, dst_ref=dst, send_sem=send, recv_sem=recv,
                device_id=target, device_id_type=MESH,
            )

        def arrived(dst, send, recv):
            copy(dst, dst, send, recv, sibling).wait_recv()

        def sent(src, send, recv):
            copy(src, src, send, recv, sibling).wait_send()

        def cols(h):
            return pl.ds(pl.multiple_of(h * HD, HD), HD)

        far_first = sorted(range(1, NY), key=lambda d: -min(d, NY - d))
        own = [
            pltpu.make_async_copy(k_ref.at[:, cols(head)], kvbuf.at[0, mine, c, :, pl.ds(0, HD)], own_s.at[0]),
            pltpu.make_async_copy(v_ref.at[:, cols(head)], kvbuf.at[0, mine, c, :, pl.ds(HD, HD)], own_s.at[1]),
            pltpu.make_async_copy(q_ref.at[:, cols(head)], qbuf.at[y], own_s.at[2]),
            pltpu.make_async_copy(gates_ref, gates, own_s.at[3]),
            pltpu.make_async_copy(cot_ref, cots, own_s.at[4]),
            pltpu.make_async_copy(lengths, counts, own_s.at[5]),
            pltpu.make_async_copy(gain_ref, gains, own_s.at[6]),
            pltpu.make_async_copy(bias_ref, biases, own_s.at[7]),
        ]
        for one in own:
            one.start()

        def store(index, here, there):
            pltpu.make_async_copy(here, there, out_s.at[index]).start()

        barrier = pltpu.get_barrier_semaphore()
        partners = [at(x, (y + d) % NY, c) for d in range(1, NY)]
        partners += [at((x + d) % NX, y, c) for d in range(1, NX)]
        partners += [sibling]
        for partner in partners:
            pl.semaphore_signal(barrier, inc=1, device_id=partner, device_id_type=MESH)

        @pl.when(z == 0)
        def _():
            for d in range(1, nz):
                pl.semaphore_signal(barrier, inc=1, device_id={"dp": d}, device_id_type=MESH)

        pl.semaphore_wait(barrier, len(partners) + jnp.where(z == 0, 0, 1))

        for d in far_first:
            if d % 2:
                continue
            yy = (y + d) % NY
            copy(
                k_ref.at[:, cols(yy // 2)], kvbuf.at[0, mine, c, :, pl.ds(0, HD)],
                k_s.at[d // 2], k_r.at[mine], at(x, yy, c),
            ).start()
            copy(
                v_ref.at[:, cols(yy // 2)], kvbuf.at[0, mine, c, :, pl.ds(HD, HD)],
                v_s.at[d // 2], v_r.at[mine], at(x, yy, c),
            ).start()
        for d in far_first:
            yy = (y + d) % NY
            copy(q_ref.at[:, cols(yy // 2)], qbuf.at[y], q_s.at[d], q_r.at[y], at(x, yy, c)).start()

        def forward_block(k):
            block = kvbuf.at[0, k, c]

            @pl.when(x < NX - 1)
            def _():
                copy(block, kvbuf.at[1, k, c], f_s.at[1, k], f_r.at[1, k], at((x + 1) % NX, y, c)).start()

            @pl.when((x < NX - 2) & (k % 2 == 1))
            def _():
                copy(block, relay.at[k // 2], r_s.at[k // 2], r_r.at[k // 2], at((x + NX - 1) % NX, y, c)).start()

        def forward_again(block, k, target):
            copy(block, kvbuf.at[2, k, c], f_s.at[2, k], f_r.at[2, k], at(target, y, c)).start()

        def share_block(t, k):
            block = kvbuf.at[t, k, c]
            copy(block, block, f_s.at[3 + t, k], f_r.at[3 + t, k], sibling).start()

        def share_stripe(t):
            @pl.when(x >= t)
            def _():
                for k in range(pairs):
                    arrived(kvbuf.at[t, k, c], f_s.at[t, k], f_r.at[t, k])
                    share_block(t, k)
                    if t == 1 and k % 2 == 0:
                        @pl.when(x < NX - 1)
                        def _(k=k):
                            forward_again(kvbuf.at[1, k, c], k, (x + 1) % NX)

        def shared(t):
            for k in range(pairs):
                arrived(kvbuf.at[t, k, 1 - c], f_s.at[3 + t, k], f_r.at[3 + t, k])

        for i in (5, 6, 7):
            own[i].wait()
        ends = []
        running = jnp.int32(0)
        for u in range(USERS):
            running = running + counts[0, u]
            ends.append(running)
        for slot in range(NY):
            block = stripe * x + 2 * slot + c
            begin = jnp.int32(0)
            final = jnp.int32(0)
            for end in ends:
                begin = jnp.maximum(begin, jnp.where(end <= block, end, 0))
                final = jnp.maximum(final, jnp.where(end == block + 1, 1, 0))
            marks[0, slot] = begin * rows
            marks[1, slot] = jnp.where(final == 1, block, 2 * NX * stripe) * rows

        own[0].wait()
        own[1].wait()
        share_block(0, mine)
        forward_block(mine)
        for d in range(1, pairs):
            k = (mine + d) % pairs
            arrived(kvbuf.at[0, k, c, :, pl.ds(0, HD)], k_s.at[0], k_r.at[k])
            arrived(kvbuf.at[0, k, c, :, pl.ds(HD, HD)], v_s.at[0], v_r.at[k])
            share_block(0, k)
            forward_block(k)

        @pl.when((x == 0) | (x == NX - 1))
        def _():
            for i in range(halves):
                arrived(relay.at[i], r_s.at[i], r_r.at[i])
                forward_again(relay.at[i], 2 * i + 1, (x + NX - 1) % NX)

        share_stripe(1)

        column = lax.broadcasted_iota(jnp.int32, (1, tile_k), 1)
        column = (column // (2 * rows)) * (4 * rows) + column % (2 * rows)
        grid_row = lax.broadcasted_iota(jnp.int32, (tile_q, tile_k), 0)
        grid_column = lax.broadcasted_iota(jnp.int32, (tile_q, tile_k), 1)
        grid_gap = (
            (grid_column // (2 * rows)) * (4 * rows) + grid_column % (2 * rows)
            - grid_row - jnp.where(grid_row >= rows, rows, 0)
        )

        def keys_of(t, half):
            return kvbuf[t, 2 * half:2 * half + 2, :, :, 0:HD].reshape(tile_k, HD)

        def values_of(t, half):
            return kvbuf[t, 2 * half:2 * half + 2, :, :, HD:2 * HD].reshape(tile_k, HD)

        def forward_tile(t, m, half):
            shift = (2 * par + 8 * half) * rows
            at_key = column + (stripe * (x - t) * rows + shift)
            inside = []
            for slot in (2 * m, 2 * m + 1):
                kept = at_key >= marks[0, slot]
                if t == 0 and half == m // 2:
                    kept = kept & (at_key < marks[1, slot])
                inside.append(jnp.broadcast_to(jnp.where(kept, 1.0, 0.0), (rows, tile_k)))
            inside = jnp.concatenate(inside, axis=0)
            if t == 0 and half == m // 2:
                gap = grid_gap + (shift - (c + 4 * m) * rows)
                inside = jnp.where(gap < 0, inside, jnp.where(gap == 0, 1.0, 0.0))
            queries = qbuf[2 * m:2 * m + 2].reshape(tile_q, HD)
            small = dot_t(queries, keys_of(t, half)) * (0.5 * scale)
            twice = jnp.tanh(small) + 1.0
            weighed = twice * inside
            prob = small * weighed
            slot = (t * 2 + m % 2) * halves + half
            place = slice((m // 2) * tile_q, (m // 2 + 1) * tile_q)
            prob_low = prob.astype(BF16)
            probs[slot, place] = prob_low
            derivs[slot, place] = (weighed + prob * (2.0 - twice)).astype(BF16)
            return dot(prob_low, values_of(t, half))

        def spans(t, m):
            if t == 0:
                return range(0, m // 2 + 1)
            if t == 1:
                return range(0, halves)
            return range(m // 2, halves)

        def forward_side(t, side):
            for m in range(side, pairs, 2):
                result = None
                for half in spans(t, m):
                    part = forward_tile(t, m, half)
                    result = part if result is None else result + part
                att_acc[m] = result if t == 0 else att_acc[m] + result

        def to_owner(slot, source, landing, send, recv):
            there = landing.at[par, :, cols(head)]

            @pl.when(slot == y)
            def _():
                landing[par, :, cols(head)] = source[slot]

            @pl.when(slot != y)
            def _():
                copy(source.at[slot], there, send.at[slot], recv.at[y], at(x, slot, c)).start()

        def to_owners(side, source, landing, send, recv):
            for far in (1, 0):
                for i in range(2):
                    slot = (y // 4 + far) % 2 * 4 + 2 * side + (y + i) % 2
                    to_owner(slot, source, landing, send, recv)

        def attended_side(side):
            for m in range(side, pairs, 2):
                att_out[2 * m] = att_acc[m, 0:rows].astype(BF16)
                att_out[2 * m + 1] = att_acc[m, rows:2 * rows].astype(BF16)
            to_owners(side, att_out, att_in, att_s, att_r)

        def queries_here(side):
            for slot in range(4 * side, 4 * side + 4):
                @pl.when(slot == y)
                def _():
                    own[2].wait()

                @pl.when(slot != y)
                def _(slot=slot):
                    arrived(qbuf.at[slot], q_s.at[0], q_r.at[slot])

        queries_here(0)
        queries_here(1)
        shared(0)
        forward_side(0, 0)
        forward_side(0, 1)

        @pl.when(x >= 1)
        def _():
            shared(1)
            forward_side(1, 0)

        share_stripe(2)

        @pl.when(x >= 1)
        def _():
            forward_side(1, 1)

        @pl.when(x >= 2)
        def _():
            shared(2)
            forward_side(2, 0)

        attended_side(0)

        @pl.when(x >= 2)
        def _():
            forward_side(2, 1)

        attended_side(1)

        def transposed(source, target):
            for m in range(pairs):
                block = source[2 * m:2 * m + 2].reshape(tile_q, HD)
                target[m % 2, :, (m // 2) * tile_q:(m // 2 + 1) * tile_q] = block.T

        def gather_owner(landing, send, recv):
            for d in range(1, NY):
                yy = (y + d) % NY
                arrived(landing.at[yy % 2, :, cols(yy // 2)], send.at[0], recv.at[yy])

        def spread(buf, index, count, send, recv, target):
            for d in range(1, count):
                copy(buf.at[index], buf.at[index], send.at[d], recv.at[index], target(d)).start()

        def total(buf, index, count, send, recv):
            for d in range(1, count):
                other = (index + d) % count
                arrived(buf.at[other], send.at[0], recv.at[other])
            result = buf[0]
            for i in range(1, count):
                result = result + buf[i]
            return result

        dq_acc[...] = jnp.zeros_like(dq_acc)
        transposed(qbuf, q_t)
        own[3].wait()
        own[4].wait()
        gain = gains[...]
        cot = cots[...].astype(F32)
        upstream = cot * gates[...].astype(F32)
        dnormal = upstream * gain
        dnormal_mean = jnp.mean(dnormal, axis=-1, keepdims=True)
        ysum[y, 1:2] = jnp.sum(upstream, axis=0, keepdims=True)

        gather_owner(att_in, att_s, att_r)
        attended = att_in[0].astype(F32) + att_in[1].astype(F32)
        mean = jnp.mean(attended, axis=-1, keepdims=True)
        centered = attended - mean
        variance = jnp.mean(centered * centered, axis=-1, keepdims=True)
        inverse = lax.rsqrt(variance + EPS)
        normal = centered * inverse
        grad_att = inverse * (
            dnormal - dnormal_mean - normal * jnp.mean(dnormal * normal, axis=-1, keepdims=True)
        )
        up[...] = grad_att.astype(BF16)
        ysum[y, 0:1] = jnp.sum(upstream * normal, axis=0, keepdims=True)
        spread(ysum, y, NY, ys_s, ys_r, lambda d: at(x, (y + d) % NY, c))
        for d in far_first:
            yy = (y + d) % NY
            copy(up.at[:, cols(yy // 2)], dabuf.at[y], da_s.at[d], da_r.at[y], at(x, yy, c)).start()
        dabuf[y] = up[:, cols(head)]
        gg_out[...] = (cot * (normal * gain + biases[...])).astype(BF16)
        store(3, gg_out, gg_ref)

        xsum[x] = total(ysum, y, NY, ys_s, ys_r)
        spread(xsum, x, NX, xs_s, xs_r, lambda d: at((x + d) % NX, y, c))

        for d in range(1, NY):
            slot = (y + d) % NY
            arrived(dabuf.at[slot], da_s.at[0], da_r.at[slot])
        transposed(dabuf, da_t)

        def backward_tile(t, side, half):
            slot = (t * 2 + side) * halves + half
            ms = [m for m in (side, side + 2) if half in spans(t, m)]
            span = slice(ms[0] // 2 * tile_q, (ms[-1] // 2 + 1) * tile_q)
            ups = jnp.concatenate([dabuf[2 * m:2 * m + 2].reshape(tile_q, HD) for m in ms], axis=0)
            pressure = dot_t(ups, values_of(t, half))
            grads = (pressure * derivs[slot, span].astype(F32)).astype(BF16)
            dq_acc[side, span] += dot(grads, keys_of(t, half))
            part_k = dot(q_t[side, :, span], grads)
            part_v = dot(da_t[side, :, span], probs[slot, span])
            if side == 0:
                dk_t[t, half, 0:HD] = part_k
                dk_t[t, half, HD:2 * HD] = part_v
            else:
                dk_t[t, half, 0:HD] += part_k
                dk_t[t, half, HD:2 * HD] += part_v

        def split_cores(t, half):
            for k in (2 * half, 2 * half + 1):
                there = slice((k % 2) * 2 * rows, (k % 2 + 1) * 2 * rows)
                part = jnp.concatenate(
                    [(dk_t[t, half, 0:HD, there] * (0.5 * scale)).T, dk_t[t, half, HD:2 * HD, there].T], axis=1
                )
                upper, lower = part[0:rows], part[rows:2 * rows]

                @pl.when(c == 0)
                def _(k=k, upper=upper, lower=lower):
                    keep[t, k] = upper
                    sib_out[t, k] = lower.astype(BF16)

                @pl.when(c == 1)
                def _(k=k, upper=upper, lower=lower):
                    keep[t, k] = lower
                    sib_out[t, k] = upper.astype(BF16)

            some = pl.ds(2 * half, 2)
            copy(sib_out.at[t, some], sib_in.at[t, some], sib_s.at[t, half], sib_r.at[t, half], sibling).start()

        turn = mine % 2

        def summed(t, k):
            return keep[t, k] + sib_in[t, k].astype(F32)

        def sibling_here(t, half):
            some = pl.ds(2 * half, 2)
            arrived(sib_in.at[t, some], sib_s.at[t, half], sib_r.at[t, half])

        def back_two(half):
            sibling_here(2, half)
            odd = 2 * half + turn
            even = 2 * half + 1 - turn
            x_out[1, even] = summed(2, even).astype(BF16)
            x_out[1, odd] = summed(2, odd).astype(BF16)
            copy(x_out.at[1, even], mid_in.at[half], xo_s.at[1, even], mid_r.at[half], at((x + NX - 1) % NX, y, c)).start()
            copy(x_out.at[1, odd], pass_in.at[half], xo_s.at[1, odd], pass_r.at[half], at((x + 1) % NX, y, c)).start()

        def back_one(k):
            copy(x_out.at[0, k], x_in.at[0, k], xo_s.at[0, k], xo_r.at[0, k], at((x + NX - 1) % NX, y, c)).start()

        def back_odd(half):
            sibling_here(1, half)
            odd = 2 * half + turn
            x_out[0, odd] = summed(1, odd).astype(BF16)
            back_one(odd)

        def back_even(half):
            even = 2 * half + 1 - turn
            keep[1, even] = summed(1, even)

            @pl.when(x < NX - 1)
            def _():
                arrived(mid_in.at[half], xo_s.at[1, 0], mid_r.at[half])
                keep[1, even] += mid_in[half].astype(F32)

            x_out[0, even] = keep[1, even].astype(BF16)
            back_one(even)

        def pass_back(half):
            arrived(pass_in.at[half], xo_s.at[1, 0], pass_r.at[half])
            copy(
                pass_in.at[half], x_in.at[1, 2 * half + turn], pass_s.at[half], xo_r.at[1, 2 * half + turn],
                at((x + 1) % NX, y, c),
            ).start()

        def grad_queries_side(side):
            for m in range(side, pairs, 2):
                first = (m // 2) * tile_q
                part = dq_acc[side, first:first + rows] * (0.5 * scale)
                dq_out[2 * m] = part.astype(BF16)
                part = dq_acc[side, first + rows:first + 2 * rows] * (0.5 * scale)
                dq_out[2 * m + 1] = part.astype(BF16)
            to_owners(side, dq_out, dq_in, dq_s, dq_r)

        @pl.when(x >= 2)
        def _():
            for half in range(halves):
                backward_tile(2, 0, half)
                backward_tile(2, 1, half)
                split_cores(2, half)
            back_two(0)

        csum[c] = total(xsum, x, NX, xs_s, xs_r)
        spread(csum, c, 2, cs_s, cs_r, lambda d: sibling)

        @pl.when(x >= 1)
        def _():
            backward_tile(1, 0, 0)
            backward_tile(1, 1, 0)
            split_cores(1, 0)

        @pl.when(x >= 2)
        def _():
            back_two(1)

        @pl.when(x >= 1)
        def _():
            backward_tile(1, 0, 1)
            backward_tile(1, 1, 1)
            split_cores(1, 1)
            back_odd(0)

        zsum[z] = total(csum, c, 2, cs_s, cs_r)

        @pl.when(z > 0)
        def _():
            copy(zsum.at[z], zsum.at[z], zs_s.at[0], zs_r.at[z], {"dp": 0}).start()

        backward_tile(0, 0, 0)
        backward_tile(0, 0, 1)
        grad_queries_side(0)

        @pl.when(x >= 1)
        def _():
            back_odd(1)
            back_even(0)

        @pl.when((x == 0) | (x == NX - 1))
        def _():
            pass_back(0)

        backward_tile(0, 1, 0)
        split_cores(0, 0)

        @pl.when(x >= 1)
        def _():
            back_even(1)

        @pl.when((x == 0) | (x == NX - 1))
        def _():
            pass_back(1)

        backward_tile(0, 1, 1)
        split_cores(0, 1)
        grad_queries_side(1)

        for half in range(halves):
            some = pl.ds(2 * half, 2)
            arrived(sib_in.at[0, some], sib_s.at[0, half], sib_r.at[0, half])
            keep[0, some] = keep[0, some] + sib_in[0, some].astype(F32)

        for odd in (1, 0):
            for half in range(halves):
                k = (mine + 2 * half + 2 + 1 - odd) % pairs

                @pl.when(x < NX - 1)
                def _(k=k):
                    arrived(x_in.at[0, k], xo_s.at[0, k], xo_r.at[0, k])
                    keep[0, k] += x_in[0, k].astype(F32)

                if odd:
                    @pl.when(x < NX - 2)
                    def _(k=k):
                        arrived(x_in.at[1, k], xo_s.at[1, k], xo_r.at[1, k])
                        keep[0, k] += x_in[1, k].astype(F32)

                fin[k] = keep[0, k].astype(BF16)
                yy = par + 2 * k

                @pl.when(k == mine)
                def _(k=k):
                    pltpu.make_async_copy(fin.at[k, :, pl.ds(0, HD)], gk_ref.at[:, cols(head)], out_s.at[1]).start()
                    pltpu.make_async_copy(fin.at[k, :, pl.ds(HD, HD)], gv_ref.at[:, cols(head)], out_s.at[2]).start()

                @pl.when(k != mine)
                def _(k=k, yy=yy):
                    copy(fin.at[k, :, pl.ds(0, HD)], gk_ref.at[:, cols(head)], fk_s.at[k], fk_r.at[head], at(x, yy, c)).start()
                    copy(fin.at[k, :, pl.ds(HD, HD)], gv_ref.at[:, cols(head)], fv_s.at[k], fv_r.at[head], at(x, yy, c)).start()

        @pl.when(z == 0)
        def _():
            result = zsum[0]
            for i in range(1, nz):
                arrived(zsum.at[i], zs_s.at[0], zs_r.at[i])
                result = result + zsum[i]
            gn_out[...] = result * norm_scale
            store(4, gn_out, gn_ref)
            for i in range(1, nz):
                copy(gn_out, gn_ref, zs_s.at[i], gn_r.at[0], {"dp": i}).start()

        gather_owner(dq_in, dq_s, dq_r)
        gq_out[...] = (dq_in[0].astype(F32) + dq_in[1].astype(F32)).astype(BF16)
        store(0, gq_out, gq_ref)


        for d in range(2, NY, 2):
            sent(k_ref.at[:, cols(head)], k_s.at[d // 2], k_r.at[0])
            sent(v_ref.at[:, cols(head)], v_s.at[d // 2], v_r.at[0])
        for d in range(1, NY):
            sent(qbuf.at[0], q_s.at[d], q_r.at[0])
            sent(dabuf.at[0], da_s.at[d], da_r.at[0])
            slot = (y + d) % NY
            sent(att_out.at[slot], att_s.at[slot], att_r.at[0])
            sent(dq_out.at[slot], dq_s.at[slot], dq_r.at[0])
            sent(ysum.at[y], ys_s.at[d], ys_r.at[0])
        for k in range(pairs):
            sent(kvbuf.at[0, k, c], f_s.at[3, k], f_r.at[0, k])

        @pl.when(x < NX - 1)
        def _():
            for k in range(pairs):
                sent(kvbuf.at[0, k, c], f_s.at[1, k], f_r.at[0, k])

        @pl.when(x < NX - 2)
        def _():
            for i in range(halves):
                sent(relay.at[i], r_s.at[i], r_r.at[i])

        @pl.when((x == 0) | (x == NX - 1))
        def _():
            for half in range(halves):
                sent(pass_in.at[half], pass_s.at[half], pass_r.at[half])
            for k in range(1, pairs, 2):
                sent(kvbuf.at[0, k, c], f_s.at[2, k], f_r.at[0, k])

        @pl.when((x > 0) & (x < NX - 1))
        def _():
            for k in range(0, pairs, 2):
                sent(kvbuf.at[0, k, c], f_s.at[2, k], f_r.at[0, k])

        for t in (1, 2):
            @pl.when(x >= t)
            def _(t=t):
                for k in range(pairs):
                    sent(kvbuf.at[t, k, c], f_s.at[3 + t, k], f_r.at[0, k])
                for half in range(halves):
                    some = pl.ds(2 * half, 2)
                    sent(sib_out.at[t, some], sib_s.at[t, half], sib_r.at[t, half])
                for k in range(pairs):
                    sent(x_out.at[t - 1, k], xo_s.at[t - 1, k], xo_r.at[t - 1, k])
        for half in range(halves):
            some = pl.ds(2 * half, 2)
            sent(sib_out.at[0, some], sib_s.at[0, half], sib_r.at[0, half])
        for d in range(1, NX):
            sent(xsum.at[x], xs_s.at[d], xs_r.at[0])
        sent(csum.at[c], cs_s.at[1], cs_r.at[0])

        @pl.when(z > 0)
        def _():
            sent(zsum.at[z], zs_s.at[0], zs_r.at[0])

        @pl.when(z == 0)
        def _():
            for i in range(1, nz):
                sent(gn_out, zs_s.at[i], zs_r.at[0])

        for d in range(1, heads):
            h = (head + d) % heads
            arrived(gk_ref.at[:, cols(h)], fk_s.at[0], fk_r.at[h])
            arrived(gv_ref.at[:, cols(h)], fv_s.at[0], fv_r.at[h])
        @pl.when(z > 0)
        def _():
            arrived(gn_ref, zs_s.at[0], gn_r.at[0])

        @pl.when(z == 0)
        def _():
            pltpu.make_async_copy(gn_out, gn_ref, out_s.at[4]).wait()

        for d in range(1, pairs):
            k = (mine + d) % pairs
            sent(fin.at[k, :, pl.ds(0, HD)], fk_s.at[k], fk_r.at[0])
            sent(fin.at[k, :, pl.ds(HD, HD)], fv_s.at[k], fv_r.at[0])
        for i, (here, there) in enumerate(
            [
                (gq_out, gq_ref),
                (fin.at[mine, :, pl.ds(0, HD)], gk_ref.at[:, cols(head)]),
                (fin.at[mine, :, pl.ds(HD, HD)], gv_ref.at[:, cols(head)]),
                (gg_out, gg_ref),
            ]
        ):
            pltpu.make_async_copy(here, there, out_s.at[i]).wait()

    vm = pltpu.VMEM
    sem = pltpu.SemaphoreType.DMA
    scratch = [
        vm((NY, rows, HD), BF16),
        vm((3, pairs, 2, rows, 2 * HD), BF16),
        vm((rows, width), BF16),
        vm((rows, width), BF16),
        vm((6 * halves, 2 * tile_q, tile_k), BF16),
        vm((6 * halves, 2 * tile_q, tile_k), BF16),
        vm((pairs, tile_q, HD), F32),
        vm((NY, rows, HD), BF16),
        vm((2, rows, width), BF16),
        vm((rows, width), BF16),
        vm((NY, rows, HD), BF16),
        vm((2, HD, 2 * tile_q), BF16),
        vm((2, HD, 2 * tile_q), BF16),
        vm((2, 2 * tile_q, HD), F32),
        vm((NY, rows, HD), BF16),
        vm((2, rows, width), BF16),
        vm((3, halves, 2 * HD, tile_k), F32),
        vm((3, pairs, rows, 2 * HD), F32),
        vm((3, pairs, rows, 2 * HD), BF16),
        vm((3, pairs, rows, 2 * HD), BF16),
        vm((2, pairs, rows, 2 * HD), BF16),
        vm((2, pairs, rows, 2 * HD), BF16),
        vm((pairs, rows, 2 * HD), BF16),
        vm((NY, 2, width), F32),
        vm((NX, 2, width), F32),
        vm((2, 2, width), F32),
        vm((nz, 2, width), F32),
        vm((rows, width), BF16),
        vm((rows, width), BF16),
        vm((2, width), F32),
        vm((1, width), F32),
        vm((1, width), F32),
        vm((halves, rows, 2 * HD), BF16),
        vm((halves, rows, 2 * HD), BF16),
        vm((halves, rows, 2 * HD), BF16),
        pltpu.SMEM((2, NY), jnp.int32),
        pltpu.SMEM((1, USERS), jnp.int32),
        sem((8,)), sem((halves,)), sem((halves,)), sem((halves,)), sem((halves,)), sem((halves,)),
        sem((NY,)), sem((NY,)),
        sem((pairs,)), sem((pairs,)), sem((pairs,)), sem((pairs,)),
        sem((6, pairs)), sem((6, pairs)),
        sem((NY,)), sem((NY,)), sem((NY,)), sem((NY,)), sem((NY,)), sem((NY,)),
        sem((3, halves)), sem((3, halves)), sem((2, pairs)), sem((2, pairs)),
        sem((pairs,)), sem((pairs,)), sem((pairs,)), sem((pairs,)),
        sem((NY,)), sem((NY,)), sem((NX,)), sem((NX,)), sem((2,)), sem((2,)), sem((nz,)), sem((nz,)), sem((1,)),
        sem((5,)),
    ]
    out = jax.ShapeDtypeStruct((rows, width), BF16)
    far = pl.BlockSpec(memory_space=pltpu.HBM)
    return pl.pallas_call(
        kernel,
        out_shape=[out, out, out, out, jax.ShapeDtypeStruct((2, width), F32)],
        in_specs=[far] * 8,
        out_specs=[far] * 5,
        scratch_shapes=scratch,
        compiler_params=pltpu.CompilerParams(
            collective_id=0, has_side_effects=True, vmem_limit_bytes=63 * 1024 * 1024
        ),
    )


def write_out(*refs):
    arrays, outs, held, sems = refs[0:5], refs[5:11], refs[11:16], refs[16]
    loads = [pltpu.make_async_copy(arrays[i], held[i], sems.at[i]) for i in range(5)]
    places = list(held[0:4]) + [held[4].at[0], held[4].at[1]]
    stores = [pltpu.make_async_copy(places[i], outs[i], sems.at[5 + i]) for i in range(6)]
    for load in loads:
        load.start()
    for i in range(4):
        loads[i].wait()
        stores[i].start()
    loads[4].wait()
    stores[4].start()
    stores[5].start()
    for store in stores:
        store.wait()


def written(*arrays):
    far = pl.BlockSpec(memory_space=pltpu.HBM)
    gn = arrays[4]
    row = jax.ShapeDtypeStruct(gn.shape[1:], gn.dtype)
    return pl.pallas_call(
        write_out,
        out_shape=[jax.ShapeDtypeStruct(one.shape, one.dtype) for one in arrays[0:4]] + [row, row],
        in_specs=[far] * 5,
        out_specs=[far] * 6,
        scratch_shapes=[pltpu.VMEM(one.shape, one.dtype) for one in arrays] + [pltpu.SemaphoreType.DMA((11,))],
        compiler_params=pltpu.CompilerParams(vmem_limit_bytes=63 * 1024 * 1024),
    )(*arrays)


def solution(mesh):
    nz = mesh.shape["dp"]

    def per_device(queries, keys, values, gates, cotangent, lengths, gain, bias):
        gq, gk, gv, gg, gn = make_kernel(nz, queries.shape[1])(
            lengths, queries[0], keys[0], values[0], gates[0], cotangent[0], gain[None], bias[None]
        )
        gq, gk, gv, gg, gain_grad, bias_grad = written(gq, gk, gv, gg, gn)
        return gq[None], gk[None], gv[None], gg[None], gain_grad, bias_grad

    rows = P("dp", "seq", None)
    return jax.shard_map(
        per_device,
        mesh=mesh,
        in_specs=(rows, rows, rows, rows, rows, P("dp", None), P(), P()),
        out_specs=(rows, rows, rows, rows, P(), P()),
        check_vma=False,
    )
```

```python
import math

import jax
import jax.numpy as jnp
from jax import lax
from jax.experimental import pallas as pl
from jax.experimental.pallas import tpu as pltpu
from jax.sharding import PartitionSpec as P

MESH = pl.DeviceIdType.MESH
NX = 4
NY = 8
HD = 128
EPS = 1e-05
USERS = 5

F32 = jnp.float32
BF16 = jnp.bfloat16


def dot(a, b):
    return lax.dot_general(a, b, (((1,), (0,)), ((), ())), preferred_element_type=F32)


def dot_t(a, b):
    return lax.dot_general(a, b, (((1,), (1,)), ((), ())), preferred_element_type=F32)


def make_kernel(nz, rows):
    pairs = NY // 2
    halves = pairs // 2
    stripe = 2 * NY
    heads = NY // 2
    width = heads * HD
    tile_q = 2 * rows
    tile_k = 4 * rows
    scale = HD ** (-0.5)
    norm_scale = 1.0 / math.sqrt(nz * NX * stripe * rows)

    def kernel(
        lengths, q_ref, k_ref, v_ref, gates_ref, cot_ref, gain_ref, bias_ref,
        gq_ref, gk_ref, gv_ref, gg_ref, gn_ref,
        qbuf, kvbuf, gates, cots, probs, derivs, att_acc, att_out, att_in, up, dabuf, q_t, da_t,
        dq_acc, dq_out, dq_in, dk_t, keep, sib_out, sib_in, x_out, x_in, fin,
        ysum, xsum, csum, zsum, gq_out, gg_out, gn_out, gains, biases, relay, mid_in, pass_in, marks, counts,
        own_s, r_s, r_r, mid_r, pass_s, pass_r, q_s, q_r, k_s, k_r, v_s, v_r, f_s, f_r, att_s, att_r, da_s, da_r, dq_s, dq_r,
        sib_s, sib_r, xo_s, xo_r, fk_s, fk_r, fv_s, fv_r,
        ys_s, ys_r, xs_s, xs_r, cs_s, cs_r, zs_s, zs_r, gn_r, out_s,
    ):
        me = lax.axis_index("seq")
        z = lax.axis_index("dp")
        x = me // stripe
        y = (me % stripe) // 2
        c = me % 2
        head = y // 2
        par = y % 2
        mine = y // 2

        def at(xx, yy, cc):
            return {"seq": (xx * NY + yy) * 2 + cc}

        sibling = at(x, y, 1 - c)

        def copy(src, dst, send, recv, target):
            return pltpu.make_async_remote_copy(
                src_ref=src, dst_ref=dst, send_sem=send, recv_sem=recv,
                device_id=target, device_id_type=MESH,
            )

        def arrived(dst, send, recv):
            copy(dst, dst, send, recv, sibling).wait_recv()

        def sent(src, send, recv):
            copy(src, src, send, recv, sibling).wait_send()

        def cols(h):
            return pl.ds(pl.multiple_of(h * HD, HD), HD)

        far_first = sorted(range(1, NY), key=lambda d: -min(d, NY - d))
        own = [
            pltpu.make_async_copy(k_ref.at[:, cols(head)], kvbuf.at[0, mine, c, :, pl.ds(0, HD)], own_s.at[0]),
            pltpu.make_async_copy(v_ref.at[:, cols(head)], kvbuf.at[0, mine, c, :, pl.ds(HD, HD)], own_s.at[1]),
            pltpu.make_async_copy(q_ref.at[:, cols(head)], qbuf.at[y], own_s.at[2]),
            pltpu.make_async_copy(gates_ref, gates, own_s.at[3]),
            pltpu.make_async_copy(cot_ref, cots, own_s.at[4]),
            pltpu.make_async_copy(lengths, counts, own_s.at[5]),
            pltpu.make_async_copy(gain_ref, gains, own_s.at[6]),
            pltpu.make_async_copy(bias_ref, biases, own_s.at[7]),
        ]
        for one in own:
            one.start()

        def store(index, here, there):
            pltpu.make_async_copy(here, there, out_s.at[index]).start()

        barrier = pltpu.get_barrier_semaphore()
        partners = [at(x, (y + d) % NY, c) for d in range(1, NY)]
        partners += [at((x + d) % NX, y, c) for d in range(1, NX)]
        partners += [sibling]
        for partner in partners:
            pl.semaphore_signal(barrier, inc=1, device_id=partner, device_id_type=MESH)

        @pl.when(z == 0)
        def _():
            for d in range(1, nz):
                pl.semaphore_signal(barrier, inc=1, device_id={"dp": d}, device_id_type=MESH)

        pl.semaphore_wait(barrier, len(partners) + jnp.where(z == 0, 0, 1))

        for d in far_first:
            if d % 2:
                continue
            yy = (y + d) % NY
            copy(
                k_ref.at[:, cols(yy // 2)], kvbuf.at[0, mine, c, :, pl.ds(0, HD)],
                k_s.at[d // 2], k_r.at[mine], at(x, yy, c),
            ).start()
            copy(
                v_ref.at[:, cols(yy // 2)], kvbuf.at[0, mine, c, :, pl.ds(HD, HD)],
                v_s.at[d // 2], v_r.at[mine], at(x, yy, c),
            ).start()
        for d in far_first:
            yy = (y + d) % NY
            copy(q_ref.at[:, cols(yy // 2)], qbuf.at[y], q_s.at[d], q_r.at[y], at(x, yy, c)).start()

        def forward_block(k):
            block = kvbuf.at[0, k, c]

            @pl.when(x < NX - 1)
            def _():
                copy(block, kvbuf.at[1, k, c], f_s.at[1, k], f_r.at[1, k], at((x + 1) % NX, y, c)).start()

            @pl.when((x < NX - 2) & (k % 2 == 1))
            def _():
                copy(block, relay.at[k // 2], r_s.at[k // 2], r_r.at[k // 2], at((x + NX - 1) % NX, y, c)).start()

        def forward_again(block, k, target):
            copy(block, kvbuf.at[2, k, c], f_s.at[2, k], f_r.at[2, k], at(target, y, c)).start()

        def share_block(t, k):
            block = kvbuf.at[t, k, c]
            copy(block, block, f_s.at[3 + t, k], f_r.at[3 + t, k], sibling).start()

        def share_stripe(t):
            @pl.when(x >= t)
            def _():
                for k in range(pairs):
                    arrived(kvbuf.at[t, k, c], f_s.at[t, k], f_r.at[t, k])
                    share_block(t, k)
                    if t == 1 and k % 2 == 0:
                        @pl.when(x < NX - 1)
                        def _(k=k):
                            forward_again(kvbuf.at[1, k, c], k, (x + 1) % NX)

        def shared(t):
            for k in range(pairs):
                arrived(kvbuf.at[t, k, 1 - c], f_s.at[3 + t, k], f_r.at[3 + t, k])

        for i in (5, 6, 7):
            own[i].wait()
        ends = []
        running = jnp.int32(0)
        for u in range(USERS):
            running = running + counts[0, u]
            ends.append(running)
        for slot in range(NY):
            block = stripe * x + 2 * slot + c
            begin = jnp.int32(0)
            final = jnp.int32(0)
            for end in ends:
                begin = jnp.maximum(begin, jnp.where(end <= block, end, 0))
                final = jnp.maximum(final, jnp.where(end == block + 1, 1, 0))
            marks[0, slot] = begin * rows
            marks[1, slot] = jnp.where(final == 1, block, 2 * NX * stripe) * rows

        own[0].wait()
        own[1].wait()
        share_block(0, mine)
        forward_block(mine)
        for d in range(1, pairs):
            k = (mine + d) % pairs
            arrived(kvbuf.at[0, k, c, :, pl.ds(0, HD)], k_s.at[0], k_r.at[k])
            arrived(kvbuf.at[0, k, c, :, pl.ds(HD, HD)], v_s.at[0], v_r.at[k])
            share_block(0, k)
            forward_block(k)

        @pl.when((x == 0) | (x == NX - 1))
        def _():
            for i in range(halves):
                arrived(relay.at[i], r_s.at[i], r_r.at[i])
                forward_again(relay.at[i], 2 * i + 1, (x + NX - 1) % NX)

        share_stripe(1)

        column = lax.broadcasted_iota(jnp.int32, (1, tile_k), 1)
        column = (column // (2 * rows)) * (4 * rows) + column % (2 * rows)
        grid_row = lax.broadcasted_iota(jnp.int32, (tile_q, tile_k), 0)
        grid_column = lax.broadcasted_iota(jnp.int32, (tile_q, tile_k), 1)
        grid_gap = (
            (grid_column // (2 * rows)) * (4 * rows) + grid_column % (2 * rows)
            - grid_row - jnp.where(grid_row >= rows, rows, 0)
        )

        def keys_of(t, half):
            return kvbuf[t, 2 * half:2 * half + 2, :, :, 0:HD].reshape(tile_k, HD)

        def values_of(t, half):
            return kvbuf[t, 2 * half:2 * half + 2, :, :, HD:2 * HD].reshape(tile_k, HD)

        def forward_tile(t, m, half):
            shift = (2 * par + 8 * half) * rows
            at_key = column + (stripe * (x - t) * rows + shift)
            inside = []
            for slot in (2 * m, 2 * m + 1):
                kept = at_key >= marks[0, slot]
                if t == 0 and half == m // 2:
                    kept = kept & (at_key < marks[1, slot])
                inside.append(jnp.broadcast_to(jnp.where(kept, 1.0, 0.0), (rows, tile_k)))
            inside = jnp.concatenate(inside, axis=0)
            if t == 0 and half == m // 2:
                gap = grid_gap + (shift - (c + 4 * m) * rows)
                inside = jnp.where(gap < 0, inside, jnp.where(gap == 0, 1.0, 0.0))
            queries = qbuf[2 * m:2 * m + 2].reshape(tile_q, HD)
            small = dot_t(queries, keys_of(t, half)) * (0.5 * scale)
            twice = jnp.tanh(small) + 1.0
            weighed = twice * inside
            prob = small * weighed
            slot = (t * 2 + m % 2) * halves + half
            place = slice((m // 2) * tile_q, (m // 2 + 1) * tile_q)
            prob_low = prob.astype(BF16)
            probs[slot, place] = prob_low
            derivs[slot, place] = (weighed + prob * (2.0 - twice)).astype(BF16)
            return dot(prob_low, values_of(t, half))

        def spans(t, m):
            if t == 0:
                return range(0, m // 2 + 1)
            if t == 1:
                return range(0, halves)
            return range(m // 2, halves)

        def forward_side(t, side):
            for m in range(side, pairs, 2):
                result = None
                for half in spans(t, m):
                    part = forward_tile(t, m, half)
                    result = part if result is None else result + part
                att_acc[m] = result if t == 0 else att_acc[m] + result

        def to_owner(slot, source, landing, send, recv):
            there = landing.at[par, :, cols(head)]

            @pl.when(slot == y)
            def _():
                landing[par, :, cols(head)] = source[slot]

            @pl.when(slot != y)
            def _():
                copy(source.at[slot], there, send.at[slot], recv.at[y], at(x, slot, c)).start()

        def to_owners(side, source, landing, send, recv):
            for far in (1, 0):
                for i in range(2):
                    slot = (y // 4 + far) % 2 * 4 + 2 * side + (y + i) % 2
                    to_owner(slot, source, landing, send, recv)

        def attended_side(side):
            for m in range(side, pairs, 2):
                att_out[2 * m] = att_acc[m, 0:rows].astype(BF16)
                att_out[2 * m + 1] = att_acc[m, rows:2 * rows].astype(BF16)
            to_owners(side, att_out, att_in, att_s, att_r)

        def queries_here(side):
            for slot in range(4 * side, 4 * side + 4):
                @pl.when(slot == y)
                def _():
                    own[2].wait()

                @pl.when(slot != y)
                def _(slot=slot):
                    arrived(qbuf.at[slot], q_s.at[0], q_r.at[slot])

        queries_here(0)
        queries_here(1)
        shared(0)
        forward_side(0, 0)
        forward_side(0, 1)

        @pl.when(x >= 1)
        def _():
            shared(1)
            forward_side(1, 0)

        share_stripe(2)

        @pl.when(x >= 1)
        def _():
            forward_side(1, 1)

        @pl.when(x >= 2)
        def _():
            shared(2)
            forward_side(2, 0)

        attended_side(0)

        @pl.when(x >= 2)
        def _():
            forward_side(2, 1)

        attended_side(1)

        def transposed(source, target, side):
            for m in range(side, pairs, 2):
                block = source[2 * m:2 * m + 2].reshape(tile_q, HD)
                target[m % 2, :, (m // 2) * tile_q:(m // 2 + 1) * tile_q] = block.T

        def gather_owner(landing, send, recv):
            for d in range(1, NY):
                yy = (y + d) % NY
                arrived(landing.at[yy % 2, :, cols(yy // 2)], send.at[0], recv.at[yy])

        def spread(buf, index, count, send, recv, target):
            for d in range(1, count):
                copy(buf.at[index], buf.at[index], send.at[d], recv.at[index], target(d)).start()

        def total(buf, index, count, send, recv):
            for d in range(1, count):
                other = (index + d) % count
                arrived(buf.at[other], send.at[0], recv.at[other])
            result = buf[0]
            for i in range(1, count):
                result = result + buf[i]
            return result

        dq_acc[...] = jnp.zeros_like(dq_acc)
        transposed(qbuf, q_t, 0)
        transposed(qbuf, q_t, 1)
        own[3].wait()
        own[4].wait()
        gain = gains[...]
        cot = cots[...].astype(F32)
        upstream = cot * gates[...].astype(F32)
        dnormal = upstream * gain
        dnormal_mean = jnp.mean(dnormal, axis=-1, keepdims=True)
        ysum[y, 1:2] = jnp.sum(upstream, axis=0, keepdims=True)

        gather_owner(att_in, att_s, att_r)
        attended = att_in[0].astype(F32) + att_in[1].astype(F32)
        mean = jnp.mean(attended, axis=-1, keepdims=True)
        centered = attended - mean
        variance = jnp.mean(centered * centered, axis=-1, keepdims=True)
        inverse = lax.rsqrt(variance + EPS)
        normal = centered * inverse
        grad_att = inverse * (
            dnormal - dnormal_mean - normal * jnp.mean(dnormal * normal, axis=-1, keepdims=True)
        )
        up[...] = grad_att.astype(BF16)
        ysum[y, 0:1] = jnp.sum(upstream * normal, axis=0, keepdims=True)
        spread(ysum, y, NY, ys_s, ys_r, lambda d: at(x, (y + d) % NY, c))
        for d in far_first:
            yy = (y + d) % NY
            copy(up.at[:, cols(yy // 2)], dabuf.at[y], da_s.at[d], da_r.at[y], at(x, yy, c)).start()
        dabuf[y] = up[:, cols(head)]
        gg_out[...] = (cot * (normal * gain + biases[...])).astype(BF16)
        store(3, gg_out, gg_ref)

        xsum[x] = total(ysum, y, NY, ys_s, ys_r)
        spread(xsum, x, NX, xs_s, xs_r, lambda d: at((x + d) % NX, y, c))

        def upstream_here(side):
            for slot in (2 * side, 2 * side + 1, 2 * side + 4, 2 * side + 5):
                @pl.when(slot != y)
                def _(slot=slot):
                    arrived(dabuf.at[slot], da_s.at[0], da_r.at[slot])

            transposed(dabuf, da_t, side)

        def backward_tile(t, side, half):
            slot = (t * 2 + side) * halves + half
            ms = [m for m in (side, side + 2) if half in spans(t, m)]
            span = slice(ms[0] // 2 * tile_q, (ms[-1] // 2 + 1) * tile_q)
            ups = jnp.concatenate([dabuf[2 * m:2 * m + 2].reshape(tile_q, HD) for m in ms], axis=0)
            pressure = dot_t(ups, values_of(t, half))
            grads = (pressure * derivs[slot, span].astype(F32)).astype(BF16)
            dq_acc[side, span] += dot(grads, keys_of(t, half))
            part_k = dot(q_t[side, :, span], grads)
            part_v = dot(da_t[side, :, span], probs[slot, span])
            if side == 0:
                dk_t[t, half, 0:HD] = part_k
                dk_t[t, half, HD:2 * HD] = part_v
            else:
                dk_t[t, half, 0:HD] += part_k
                dk_t[t, half, HD:2 * HD] += part_v

        def split_cores(t, half):
            for k in (2 * half, 2 * half + 1):
                there = slice((k % 2) * 2 * rows, (k % 2 + 1) * 2 * rows)
                part = jnp.concatenate(
                    [(dk_t[t, half, 0:HD, there] * (0.5 * scale)).T, dk_t[t, half, HD:2 * HD, there].T], axis=1
                )
                upper, lower = part[0:rows], part[rows:2 * rows]

                @pl.when(c == 0)
                def _(k=k, upper=upper, lower=lower):
                    keep[t, k] = upper
                    sib_out[t, k] = lower.astype(BF16)

                @pl.when(c == 1)
                def _(k=k, upper=upper, lower=lower):
                    keep[t, k] = lower
                    sib_out[t, k] = upper.astype(BF16)

            some = pl.ds(2 * half, 2)
            copy(sib_out.at[t, some], sib_in.at[t, some], sib_s.at[t, half], sib_r.at[t, half], sibling).start()

        turn = mine % 2

        def summed(t, k):
            return keep[t, k] + sib_in[t, k].astype(F32)

        def sibling_here(t, half):
            some = pl.ds(2 * half, 2)
            arrived(sib_in.at[t, some], sib_s.at[t, half], sib_r.at[t, half])

        def back_two(half):
            sibling_here(2, half)
            odd = 2 * half + turn
            even = 2 * half + 1 - turn
            x_out[1, even] = summed(2, even).astype(BF16)
            x_out[1, odd] = summed(2, odd).astype(BF16)
            copy(x_out.at[1, even], mid_in.at[half], xo_s.at[1, even], mid_r.at[half], at((x + NX - 1) % NX, y, c)).start()
            copy(x_out.at[1, odd], pass_in.at[half], xo_s.at[1, odd], pass_r.at[half], at((x + 1) % NX, y, c)).start()

        def back_one(k):
            copy(x_out.at[0, k], x_in.at[0, k], xo_s.at[0, k], xo_r.at[0, k], at((x + NX - 1) % NX, y, c)).start()

        def back_odd(half):
            sibling_here(1, half)
            odd = 2 * half + turn
            x_out[0, odd] = summed(1, odd).astype(BF16)
            back_one(odd)

        def back_even(half):
            even = 2 * half + 1 - turn
            keep[1, even] = summed(1, even)

            @pl.when(x < NX - 1)
            def _():
                arrived(mid_in.at[half], xo_s.at[1, 0], mid_r.at[half])
                keep[1, even] += mid_in[half].astype(F32)

            x_out[0, even] = keep[1, even].astype(BF16)
            back_one(even)

        def pass_back(half):
            arrived(pass_in.at[half], xo_s.at[1, 0], pass_r.at[half])
            copy(
                pass_in.at[half], x_in.at[1, 2 * half + turn], pass_s.at[half], xo_r.at[1, 2 * half + turn],
                at((x + 1) % NX, y, c),
            ).start()

        def grad_queries_side(side):
            for m in range(side, pairs, 2):
                first = (m // 2) * tile_q
                part = dq_acc[side, first:first + rows] * (0.5 * scale)
                dq_out[2 * m] = part.astype(BF16)
                part = dq_acc[side, first + rows:first + 2 * rows] * (0.5 * scale)
                dq_out[2 * m + 1] = part.astype(BF16)
            to_owners(side, dq_out, dq_in, dq_s, dq_r)

        upstream_here(0)

        @pl.when(x >= 2)
        def _():
            for half in range(halves):
                backward_tile(2, 0, half)

        @pl.when(x >= 1)
        def _():
            for half in range(halves):
                backward_tile(1, 0, half)

        for half in range(halves):
            backward_tile(0, 0, half)
        grad_queries_side(0)
        upstream_here(1)

        @pl.when(x == 1)
        def _():
            for half in range(halves):
                backward_tile(1, 1, half)
                split_cores(1, half)

        @pl.when(x <= 1)
        def _():
            for half in range(halves):
                backward_tile(0, 1, half)
                split_cores(0, half)
            grad_queries_side(1)

        @pl.when(x >= 2)
        def _():
            for half in range(halves):
                backward_tile(2, 1, half)
                split_cores(2, half)

        csum[c] = total(xsum, x, NX, xs_s, xs_r)
        spread(csum, c, 2, cs_s, cs_r, lambda d: sibling)

        @pl.when(x >= 2)
        def _():
            backward_tile(1, 1, 0)
            split_cores(1, 0)

        @pl.when(x >= 2)
        def _():
            back_two(0)
            back_two(1)

        @pl.when(x >= 2)
        def _():
            backward_tile(1, 1, 1)
            split_cores(1, 1)

        @pl.when(x >= 1)
        def _():
            back_odd(0)

        zsum[z] = total(csum, c, 2, cs_s, cs_r)

        @pl.when(z > 0)
        def _():
            copy(zsum.at[z], zsum.at[z], zs_s.at[0], zs_r.at[z], {"dp": 0}).start()

        @pl.when(x >= 2)
        def _():
            backward_tile(0, 1, 0)
            split_cores(0, 0)

        @pl.when(x >= 1)
        def _():
            back_odd(1)
            back_even(0)

        @pl.when((x == 0) | (x == NX - 1))
        def _():
            pass_back(0)

        @pl.when(x >= 2)
        def _():
            backward_tile(0, 1, 1)
            split_cores(0, 1)

        @pl.when(x >= 1)
        def _():
            back_even(1)

        @pl.when(x >= 2)
        def _():
            grad_queries_side(1)

        @pl.when((x == 0) | (x == NX - 1))
        def _():
            pass_back(1)

        for half in range(halves):
            some = pl.ds(2 * half, 2)
            arrived(sib_in.at[0, some], sib_s.at[0, half], sib_r.at[0, half])
            keep[0, some] = keep[0, some] + sib_in[0, some].astype(F32)

        for odd in (1, 0):
            for half in range(halves):
                k = (mine + 2 * half + 2 + 1 - odd) % pairs

                @pl.when(x < NX - 1)
                def _(k=k):
                    arrived(x_in.at[0, k], xo_s.at[0, k], xo_r.at[0, k])
                    keep[0, k] += x_in[0, k].astype(F32)

                if odd:
                    @pl.when(x < NX - 2)
                    def _(k=k):
                        arrived(x_in.at[1, k], xo_s.at[1, k], xo_r.at[1, k])
                        keep[0, k] += x_in[1, k].astype(F32)

                fin[k] = keep[0, k].astype(BF16)
                yy = par + 2 * k

                @pl.when(k == mine)
                def _(k=k):
                    pltpu.make_async_copy(fin.at[k, :, pl.ds(0, HD)], gk_ref.at[:, cols(head)], out_s.at[1]).start()
                    pltpu.make_async_copy(fin.at[k, :, pl.ds(HD, HD)], gv_ref.at[:, cols(head)], out_s.at[2]).start()

                @pl.when(k != mine)
                def _(k=k, yy=yy):
                    copy(fin.at[k, :, pl.ds(0, HD)], gk_ref.at[:, cols(head)], fk_s.at[k], fk_r.at[head], at(x, yy, c)).start()
                    copy(fin.at[k, :, pl.ds(HD, HD)], gv_ref.at[:, cols(head)], fv_s.at[k], fv_r.at[head], at(x, yy, c)).start()

        @pl.when(z == 0)
        def _():
            result = zsum[0]
            for i in range(1, nz):
                arrived(zsum.at[i], zs_s.at[0], zs_r.at[i])
                result = result + zsum[i]
            gn_out[...] = result * norm_scale
            store(4, gn_out, gn_ref)
            for i in range(1, nz):
                copy(gn_out, gn_ref, zs_s.at[i], gn_r.at[0], {"dp": i}).start()

        gather_owner(dq_in, dq_s, dq_r)
        gq_out[...] = (dq_in[0].astype(F32) + dq_in[1].astype(F32)).astype(BF16)
        store(0, gq_out, gq_ref)


        for d in range(2, NY, 2):
            sent(k_ref.at[:, cols(head)], k_s.at[d // 2], k_r.at[0])
            sent(v_ref.at[:, cols(head)], v_s.at[d // 2], v_r.at[0])
        for d in range(1, NY):
            sent(qbuf.at[0], q_s.at[d], q_r.at[0])
            sent(dabuf.at[0], da_s.at[d], da_r.at[0])
            slot = (y + d) % NY
            sent(att_out.at[slot], att_s.at[slot], att_r.at[0])
            sent(dq_out.at[slot], dq_s.at[slot], dq_r.at[0])
            sent(ysum.at[y], ys_s.at[d], ys_r.at[0])
        for k in range(pairs):
            sent(kvbuf.at[0, k, c], f_s.at[3, k], f_r.at[0, k])

        @pl.when(x < NX - 1)
        def _():
            for k in range(pairs):
                sent(kvbuf.at[0, k, c], f_s.at[1, k], f_r.at[0, k])

        @pl.when(x < NX - 2)
        def _():
            for i in range(halves):
                sent(relay.at[i], r_s.at[i], r_r.at[i])

        @pl.when((x == 0) | (x == NX - 1))
        def _():
            for half in range(halves):
                sent(pass_in.at[half], pass_s.at[half], pass_r.at[half])
            for k in range(1, pairs, 2):
                sent(kvbuf.at[0, k, c], f_s.at[2, k], f_r.at[0, k])

        @pl.when((x > 0) & (x < NX - 1))
        def _():
            for k in range(0, pairs, 2):
                sent(kvbuf.at[0, k, c], f_s.at[2, k], f_r.at[0, k])

        for t in (1, 2):
            @pl.when(x >= t)
            def _(t=t):
                for k in range(pairs):
                    sent(kvbuf.at[t, k, c], f_s.at[3 + t, k], f_r.at[0, k])
                for half in range(halves):
                    some = pl.ds(2 * half, 2)
                    sent(sib_out.at[t, some], sib_s.at[t, half], sib_r.at[t, half])
                for k in range(pairs):
                    sent(x_out.at[t - 1, k], xo_s.at[t - 1, k], xo_r.at[t - 1, k])
        for half in range(halves):
            some = pl.ds(2 * half, 2)
            sent(sib_out.at[0, some], sib_s.at[0, half], sib_r.at[0, half])
        for d in range(1, NX):
            sent(xsum.at[x], xs_s.at[d], xs_r.at[0])
        sent(csum.at[c], cs_s.at[1], cs_r.at[0])

        @pl.when(z > 0)
        def _():
            sent(zsum.at[z], zs_s.at[0], zs_r.at[0])

        @pl.when(z == 0)
        def _():
            for i in range(1, nz):
                sent(gn_out, zs_s.at[i], zs_r.at[0])

        for d in range(1, heads):
            h = (head + d) % heads
            arrived(gk_ref.at[:, cols(h)], fk_s.at[0], fk_r.at[h])
            arrived(gv_ref.at[:, cols(h)], fv_s.at[0], fv_r.at[h])
        @pl.when(z > 0)
        def _():
            arrived(gn_ref, zs_s.at[0], gn_r.at[0])

        @pl.when(z == 0)
        def _():
            pltpu.make_async_copy(gn_out, gn_ref, out_s.at[4]).wait()

        for d in range(1, pairs):
            k = (mine + d) % pairs
            sent(fin.at[k, :, pl.ds(0, HD)], fk_s.at[k], fk_r.at[0])
            sent(fin.at[k, :, pl.ds(HD, HD)], fv_s.at[k], fv_r.at[0])
        for i, (here, there) in enumerate(
            [
                (gq_out, gq_ref),
                (fin.at[mine, :, pl.ds(0, HD)], gk_ref.at[:, cols(head)]),
                (fin.at[mine, :, pl.ds(HD, HD)], gv_ref.at[:, cols(head)]),
                (gg_out, gg_ref),
            ]
        ):
            pltpu.make_async_copy(here, there, out_s.at[i]).wait()

    vm = pltpu.VMEM
    sem = pltpu.SemaphoreType.DMA
    scratch = [
        vm((NY, rows, HD), BF16),
        vm((3, pairs, 2, rows, 2 * HD), BF16),
        vm((rows, width), BF16),
        vm((rows, width), BF16),
        vm((6 * halves, 2 * tile_q, tile_k), BF16),
        vm((6 * halves, 2 * tile_q, tile_k), BF16),
        vm((pairs, tile_q, HD), F32),
        vm((NY, rows, HD), BF16),
        vm((2, rows, width), BF16),
        vm((rows, width), BF16),
        vm((NY, rows, HD), BF16),
        vm((2, HD, 2 * tile_q), BF16),
        vm((2, HD, 2 * tile_q), BF16),
        vm((2, 2 * tile_q, HD), F32),
        vm((NY, rows, HD), BF16),
        vm((2, rows, width), BF16),
        vm((3, halves, 2 * HD, tile_k), F32),
        vm((3, pairs, rows, 2 * HD), F32),
        vm((3, pairs, rows, 2 * HD), BF16),
        vm((3, pairs, rows, 2 * HD), BF16),
        vm((2, pairs, rows, 2 * HD), BF16),
        vm((2, pairs, rows, 2 * HD), BF16),
        vm((pairs, rows, 2 * HD), BF16),
        vm((NY, 2, width), F32),
        vm((NX, 2, width), F32),
        vm((2, 2, width), F32),
        vm((nz, 2, width), F32),
        vm((rows, width), BF16),
        vm((rows, width), BF16),
        vm((2, width), F32),
        vm((1, width), F32),
        vm((1, width), F32),
        vm((halves, rows, 2 * HD), BF16),
        vm((halves, rows, 2 * HD), BF16),
        vm((halves, rows, 2 * HD), BF16),
        pltpu.SMEM((2, NY), jnp.int32),
        pltpu.SMEM((1, USERS), jnp.int32),
        sem((8,)), sem((halves,)), sem((halves,)), sem((halves,)), sem((halves,)), sem((halves,)),
        sem((NY,)), sem((NY,)),
        sem((pairs,)), sem((pairs,)), sem((pairs,)), sem((pairs,)),
        sem((6, pairs)), sem((6, pairs)),
        sem((NY,)), sem((NY,)), sem((NY,)), sem((NY,)), sem((NY,)), sem((NY,)),
        sem((3, halves)), sem((3, halves)), sem((2, pairs)), sem((2, pairs)),
        sem((pairs,)), sem((pairs,)), sem((pairs,)), sem((pairs,)),
        sem((NY,)), sem((NY,)), sem((NX,)), sem((NX,)), sem((2,)), sem((2,)), sem((nz,)), sem((nz,)), sem((1,)),
        sem((5,)),
    ]
    out = jax.ShapeDtypeStruct((rows, width), BF16)
    far = pl.BlockSpec(memory_space=pltpu.HBM)
    return pl.pallas_call(
        kernel,
        out_shape=[out, out, out, out, jax.ShapeDtypeStruct((2, width), F32)],
        in_specs=[far] * 8,
        out_specs=[far] * 5,
        scratch_shapes=scratch,
        compiler_params=pltpu.CompilerParams(
            collective_id=0, has_side_effects=True, vmem_limit_bytes=63 * 1024 * 1024
        ),
    )


def write_out(*refs):
    arrays, outs, held, sems = refs[0:5], refs[5:11], refs[11:16], refs[16]
    loads = [pltpu.make_async_copy(arrays[i], held[i], sems.at[i]) for i in range(5)]
    places = list(held[0:4]) + [held[4].at[0], held[4].at[1]]
    stores = [pltpu.make_async_copy(places[i], outs[i], sems.at[5 + i]) for i in range(6)]
    for load in loads:
        load.start()
    for i in range(4):
        loads[i].wait()
        stores[i].start()
    loads[4].wait()
    stores[4].start()
    stores[5].start()
    for store in stores:
        store.wait()


def written(*arrays):
    far = pl.BlockSpec(memory_space=pltpu.HBM)
    gn = arrays[4]
    row = jax.ShapeDtypeStruct(gn.shape[1:], gn.dtype)
    return pl.pallas_call(
        write_out,
        out_shape=[jax.ShapeDtypeStruct(one.shape, one.dtype) for one in arrays[0:4]] + [row, row],
        in_specs=[far] * 5,
        out_specs=[far] * 6,
        scratch_shapes=[pltpu.VMEM(one.shape, one.dtype) for one in arrays] + [pltpu.SemaphoreType.DMA((11,))],
        compiler_params=pltpu.CompilerParams(vmem_limit_bytes=63 * 1024 * 1024),
    )(*arrays)


def solution(mesh):
    nz = mesh.shape["dp"]

    def per_device(queries, keys, values, gates, cotangent, lengths, gain, bias):
        gq, gk, gv, gg, gn = make_kernel(nz, queries.shape[1])(
            lengths, queries[0], keys[0], values[0], gates[0], cotangent[0], gain[None], bias[None]
        )
        gq, gk, gv, gg, gain_grad, bias_grad = written(gq, gk, gv, gg, gn)
        return gq[None], gk[None], gv[None], gg[None], gain_grad, bias_grad

    rows = P("dp", "seq", None)
    return jax.shard_map(
        per_device,
        mesh=mesh,
        in_specs=(rows, rows, rows, rows, rows, P("dp", None), P(), P()),
        out_specs=(rows, rows, rows, rows, P(), P()),
        check_vma=False,
    )
```
